256 devices in a mesh: ckpt: 8 (over y_hi, x), fsdp: 32 (over z, y_lo, core).
Axes of the slice: x: 4, y: 4 (y_hi: 2, y_lo: 2; y = y_hi * 2 + y_lo), z: 8, core: 2. Of those that a mesh axis runs over, the one named last changes fastest.
Arguments:
- states: bfloat16 [8, 16384, 768], P('ckpt', 'fsdp'), may hold values from -420 to 420
- state_tangent: bfloat16 [8, 16384, 768], P('ckpt', 'fsdp'), may hold values from -12 to 12
- loss_grad: bfloat16 [8, 16384, 768], P('ckpt', 'fsdp'), may hold values from -0.21875 to 0.21875
- norm_gain: bfloat16 [8, 768], P('ckpt'), may hold values from 0.099609375 to 1.8984375
- gain_costate: bfloat16 [8, 768], P('ckpt'), may hold values from -3 to 3
- qkv_weight: bfloat16 [8, 2304, 768], P('ckpt', 'fsdp'), may hold values from -3.1 to 3.1
- qkv_costate: bfloat16 [8, 2304, 768], P('ckpt', 'fsdp'), may hold values from -0.21875 to 0.21875
- out_weight: bfloat16 [8, 768, 768], P('ckpt', 'fsdp'), may hold values from -0.21875 to 0.21875
- out_costate: bfloat16 [8, 768, 768], P('ckpt', 'fsdp'), may hold values from -0.21875 to 0.21875
Outputs:
- scores: float32 [16384], P('fsdp')
The draws below stay inside these ranges and needn't reach their ends.
All inputs are finite; a program needn't handle non-finite values.
Results may differ from the reference program's by a relative error of at most 0.006.
The reference program's roundings to bfloat16 on the way count: a program that leaves them out, or rounds other values in their place, can miss the bound.
Values may be sent and summed in bfloat16 or wider, within the bound.
A program may use at most 64 MiB of HBM per device.

```python
import math
import jax
import jax.numpy as jnp
from jax import lax

D = 768
HEADS = 12
HEAD_DIM = 64
SEQ = 512
TOKENS = 16384
CKPTS = 8


def draw_states(key, part):
    key = jax.random.fold_in(key, 11)
    key_base, key_rows, key_cols = jax.random.split(key, 3)
    full_shape = (CKPTS, TOKENS, D)
    row_scale = jnp.exp(jax.random.uniform(key_rows, (CKPTS, TOKENS, 1), jnp.float32, 0.0, math.log(10.0)))
    col_scale = jnp.exp(jax.random.uniform(key_cols, (1, 1, D), jnp.float32, 0.0, math.log(10.0)))
    base_draw = jnp.clip(jax.random.normal(key_base, full_shape, jnp.float32), -4.0, 4.0)
    drawn_values = base_draw * row_scale * col_scale
    return drawn_values.astype(jnp.bfloat16)


def draw_qkv_weight(key, part):
    key = jax.random.fold_in(key, 23)
    key_query = jax.random.fold_in(key, 0)
    drawn_values = jnp.clip(jax.random.normal(key_query, (CKPTS, 3 * D, D), jnp.float32), -4.0, 4.0) / math.sqrt(D)
    return drawn_values.astype(jnp.bfloat16)


def levels(stream_key, extent, cuts, least, high):
    def one(dim, parts):
        steps = jax.random.uniform(jax.random.fold_in(jax.random.fold_in(stream_key, 6), dim), (parts,), jnp.float32, least / len(cuts), high / len(cuts))
        return jnp.repeat(jnp.exp(steps), extent[dim] // parts).reshape((-1,) + (1,) * (len(extent) - dim - 1))

    factor_of = one(*cuts[0])
    for cut in cuts[1:]:
        factor_of = factor_of * one(*cut)
    return factor_of


def normal_values(own_key, extent, width, limit, shards=(), kind=jnp.bfloat16):
    result = width * jax.random.normal(own_key, extent, jnp.float32)
    if shards:
        result = result * levels(own_key, extent, shards, -0.22, 0.18)
    return jnp.clip(result, -limit, limit).astype(kind)


def setup_inputs(seed: int = 0) -> dict:
    keys = jax.random.split(jax.random.key(seed), 10)
    return {
        "states": draw_states(jax.random.fold_in(keys[9], 71), 0),
        "state_tangent": normal_values(keys[1], (CKPTS, TOKENS, D), 2.0, 12.0, ((0, 8), (1, 32))),
        "loss_grad": normal_values(keys[2], (CKPTS, TOKENS, D), D ** -0.5, 0.21875, ((0, 8), (1, 32))),
        "norm_gain": jnp.clip(1.0 + 0.18 * jax.random.normal(keys[3], (CKPTS, D), jnp.float32), 0.099609375, 1.8984375).astype(jnp.bfloat16),
        "gain_costate": normal_values(keys[4], (CKPTS, D), 0.5, 3.0, ((0, 8),)),
        "qkv_weight": draw_qkv_weight(jax.random.fold_in(keys[9], 71), 0),
        "qkv_costate": normal_values(keys[6], (CKPTS, 3 * D, D), D ** -0.5, 0.21875, ((0, 8), (1, 32))),
        "out_weight": normal_values(keys[7], (CKPTS, D, D), D ** -0.5, 0.21875, ((0, 8), (1, 32))),
        "out_costate": normal_values(keys[8], (CKPTS, D, D), D ** -0.5, 0.21875, ((0, 8), (1, 32))),
    }


EPSILON = 1e-05
NEGATIVE = -1e+30

def normalize(hidden, hidden_tangent, gain_vector, gain_tangent):
    widened = hidden.astype(jnp.float32)
    widened_tangent = hidden_tangent.astype(jnp.float32)
    inverse_rms = lax.rsqrt(lax.optimization_barrier(jnp.mean(widened * widened, axis=1, keepdims=True)) + EPSILON)
    normed = widened * inverse_rms
    cross_mean = lax.optimization_barrier(jnp.mean(widened * widened_tangent, axis=1, keepdims=True))
    normed_tangent = widened_tangent * inverse_rms - widened * (inverse_rms * inverse_rms * inverse_rms) * cross_mean
    gain_wide = gain_vector.astype(jnp.float32)
    lifted = (gain_wide * normed).astype(jnp.bfloat16)
    lifted_tangent = (gain_tangent.astype(jnp.float32) * normed + gain_wide * normed_tangent).astype(jnp.bfloat16)
    return (lifted, lifted_tangent)

def dot_rows(left_side, right_side):
    return jnp.dot(left_side, right_side.T, preferred_element_type=jnp.float32)

def attend(primal, tangent, batch_count):
    model_width = primal.shape[1] // 3
    score_multiplier = 1.0 / math.sqrt(HEAD_DIM)

    def split_heads(block):
        return block.reshape(batch_count, SEQ, HEADS, HEAD_DIM).transpose(2, 0, 1, 3)
    row_index = lax.broadcasted_iota(jnp.int32, (SEQ, SEQ), 0)
    col_index = lax.broadcasted_iota(jnp.int32, (SEQ, SEQ), 1)
    causal = row_index >= col_index

    def one_head(operands):
        query_head_slice, key_head_slice, value_head_slice, query_direction, key_direction, value_direction = [item_array.astype(jnp.float32) for item_array in operands]
        attention_logits = jnp.einsum('urs,ups->urp', query_head_slice, key_head_slice) * score_multiplier
        attention_logits = jnp.where(causal, attention_logits, NEGATIVE)
        row_max = lax.optimization_barrier(jnp.max(attention_logits, axis=-1, keepdims=True))
        exponent = jnp.exp(attention_logits - row_max)
        attention = exponent / lax.optimization_barrier(jnp.sum(exponent, axis=-1, keepdims=True))
        logit_derivative = (jnp.einsum('urs,ups->urp', query_direction, key_head_slice) + jnp.einsum('urs,ups->urp', query_head_slice, key_direction)) * score_multiplier
        attention_tangent = attention * (logit_derivative - lax.optimization_barrier(jnp.sum(attention * logit_derivative, axis=-1, keepdims=True)))
        lowered_precision_weights = attention.astype(jnp.bfloat16).astype(jnp.float32)
        lowered_precision_tangent = attention_tangent.astype(jnp.bfloat16).astype(jnp.float32)
        block_output = jnp.einsum('eyo,eom->eym', lowered_precision_weights, value_head_slice)
        output_derivative = jnp.einsum('eyo,eom->eym', lowered_precision_tangent, value_head_slice) + jnp.einsum('eyo,eom->eym', lowered_precision_weights, value_direction)
        return (block_output.astype(jnp.bfloat16), output_derivative.astype(jnp.bfloat16))
    operands = (split_heads(primal[:, :model_width]), split_heads(primal[:, model_width:2 * model_width]), split_heads(primal[:, 2 * model_width:]), split_heads(tangent[:, :model_width]), split_heads(tangent[:, model_width:2 * model_width]), split_heads(tangent[:, 2 * model_width:]))
    attended, attended_tangent = lax.map(one_head, operands)

    def merge_heads(block):
        return block.transpose(1, 2, 0, 3).reshape(batch_count * SEQ, HEADS * HEAD_DIM)
    return (merge_heads(attended), merge_heads(attended_tangent))

def checkpoint_score(operands):
    hidden, hidden_tangent, gradient, gain_vector, gain_tangent, qkv_matrix, qkv_tangent, out_matrix, out_tangent_matrix = operands
    lifted, lifted_tangent = normalize(hidden, hidden_tangent, gain_vector, gain_tangent)
    primal = dot_rows(lifted, qkv_matrix).astype(jnp.bfloat16)
    tangent = (dot_rows(lifted_tangent, qkv_matrix) + dot_rows(lifted, qkv_tangent)).astype(jnp.bfloat16)
    attended, attended_tangent = attend(primal, tangent, hidden.shape[0] // SEQ)
    out_tangent = hidden_tangent.astype(jnp.float32) + dot_rows(attended_tangent, out_matrix) + dot_rows(attended, out_tangent_matrix)
    return lax.optimization_barrier(jnp.sum(gradient.astype(jnp.float32) * out_tangent, axis=1))

def reference(states, state_tangent, loss_grad, norm_gain, gain_costate, qkv_weight, qkv_costate, out_weight, out_costate):
    per_checkpoint = lax.map(checkpoint_score, (states, state_tangent, loss_grad, norm_gain, gain_costate, qkv_weight, qkv_costate, out_weight, out_costate))
    return lax.optimization_barrier(jnp.sum(per_checkpoint, axis=0))
```

```python
import functools
import math

import jax
import jax.numpy as jnp
from jax import lax
from jax.experimental import pallas as pl
from jax.experimental.pallas import tpu as pltpu
from jax.sharding import PartitionSpec as P

D = 768
HEADS = 12
HD = 64
SEQ = 512
EPSILON = 1e-05
NEGATIVE = -1e30
BF16 = jnp.bfloat16
F32 = jnp.float32
MESH = pl.DeviceIdType.MESH
NZ = 8
NCKPT = 8
NDEV = 32
RQ = 144
RO = 48

PIECES = (
    (("B", 64, 80, (64, 48), (112, 32)), ("A", 0, 64, (0, 32), (32, 32)), ("X", 0, 64, (0, 32), (32, 32))),
    (("B", 16, 32, (16, 16), (32, 16)), ("A", 0, 16, (0, 16), None), ("X", 0, 16, None, (0, 16))),
)


def dot(a, b):
    return lax.dot_general(a, b, (((1,), (0,)), ((), ())), preferred_element_type=F32)


def normalize(x_ref, t_ref, g_ref, gain_ref, cost_ref, lt_ref, ltt_ref, gt_ref, res_ref):
    gain = gain_ref[...].astype(F32)
    cost = cost_ref[...].astype(F32)

    def body(i, carry):
        rows = pl.ds(pl.multiple_of(i * 128, 128), 128)
        x = x_ref[rows, :].astype(F32)
        t = t_ref[rows, :].astype(F32)
        g = g_ref[rows, :].astype(F32)
        inv = lax.rsqrt(jnp.mean(x * x, axis=1, keepdims=True) + EPSILON)
        normed = x * inv
        cross = jnp.mean(x * t, axis=1, keepdims=True)
        normed_t = t * inv - x * (inv * inv * inv) * cross
        lifted = (gain * normed).astype(BF16)
        lifted_t = (cost * normed + gain * normed_t).astype(BF16)
        lt_ref[:, rows] = lifted.T
        ltt_ref[:, rows] = lifted_t.T
        gt_ref[:, rows] = g.T
        p = g * t
        q = p[:, 0:128]
        for k in range(1, D // 128):
            q = q + p[:, 128 * k : 128 * k + 128]
        res_ref[:, rows] = jnp.sum(q.T, axis=0, keepdims=True)
        return carry

    lax.fori_loop(0, SEQ // 128, body, 0)


def project(zc, gq_ref, lt_ref, ltt_ref, p_ref, dp_ref):
    devs = pl.ds(zc * 4, 4)
    r1 = dot(gq_ref[devs].reshape(4 * RQ, D), lt_ref[...]).reshape(4, RQ, SEQ)
    r2 = dot(gq_ref[devs, 0:80, :].reshape(320, D), ltt_ref[...]).reshape(4, 80, SEQ)
    rows = pl.ds(pl.multiple_of(zc * 288, 288), 288)
    p_ref[rows, :] = r1[:, 0:72].reshape(288, SEQ).astype(BF16)
    dp_ref[rows, :] = (r2[:, 0:72] + r1[:, 72:144]).reshape(288, SEQ).astype(BF16)


def attend_head(h, p_ref, dp_ref, at_ref, dat_ref):
    def rows(base):
        return pl.ds(pl.multiple_of(base + h * HD, HD), HD)

    q, dq = p_ref[rows(0), :], dp_ref[rows(0), :]
    k, dk = p_ref[rows(D), :], dp_ref[rows(D), :]
    v, dv = p_ref[rows(2 * D), :], dp_ref[rows(2 * D), :]
    kd = jnp.concatenate([k, dk], axis=0).T
    rhs_s = jnp.concatenate([q, jnp.zeros_like(q)], axis=0)
    rhs_d = jnp.concatenate([dq, q], axis=0)
    vv = jnp.concatenate([v, dv], axis=0)
    scale2 = math.log2(math.e) / math.sqrt(HD)
    for b in range(2):
        cols = slice(256 * b, 256 * b + 256)
        jm = 256 * (b + 1)
        s = dot(kd[:jm], rhs_s[:, cols])
        d = dot(kd[:jm], rhs_d[:, cols])
        row = lax.broadcasted_iota(jnp.int32, (256, 256), 0)
        col = lax.broadcasted_iota(jnp.int32, (256, 256), 1)
        diag = jnp.where(row <= col, s[jm - 256 :], NEGATIVE)
        s = diag if b == 0 else jnp.concatenate([s[: jm - 256], diag], axis=0)
        m = jnp.max(s, axis=0, keepdims=True)
        e = jnp.exp2((s - m) * scale2)
        r = 1.0 / jnp.sum(e, axis=0, keepdims=True)
        t = jnp.sum(e * d, axis=0, keepdims=True) * r
        a = (e * r).astype(BF16)
        da = ((e * (r * (1.0 / math.sqrt(HD)))) * (d - t)).astype(BF16)
        o1 = dot(vv[:, :jm], a)
        o2 = dot(v[:, :jm], da)
        at_ref[rows(0), cols] = o1[:HD].astype(BF16)
        dat_ref[rows(0), cols] = (o1[HD:] + o2).astype(BF16)


def out_scores(go_ref, at_ref, dat_ref, gt_ref):
    total = jnp.zeros((1, SEQ), F32)
    for b in range(2):
        devs = slice(16 * b, 16 * b + 16)
        r1 = dot(go_ref[devs, 0:32, :].reshape(512, D), dat_ref[...]).reshape(16, 32, SEQ)
        r2 = dot(go_ref[devs, 16:48, :].reshape(512, D), at_ref[...]).reshape(16, 32, SEQ)
        po = (r1[:, 0:24] + r2[:, 8:32]).reshape(384, SEQ)
        total = total + jnp.sum(po * gt_ref[384 * b : 384 * b + 384, :], axis=0, keepdims=True)
    return total


def kernel(
    x_hbm, t_hbm, g_hbm, gain_ref, cost_ref, wq_hbm, cq_hbm, wo_hbm, co_hbm,
    out_ref,
    x_ref, t_ref, g_ref, wq_ref, cq_ref, wo_ref, co_ref,
    gq_ref, go_ref, lt_ref, ltt_ref, gt_ref, res_ref, p_ref, dp_ref, at_ref, dat_ref,
    mine_ref, sums_ref,
    in_sem, ring_s, ring_r, y_s, y_r, sib_s, sib_r, sum_s, sum_r,
):
    ck = lax.axis_index("ckpt")
    me = lax.axis_index("fsdp")
    z = me // 4
    y = (me // 2) % 2
    c = me % 2

    def dev(zz, yy, cc):
        return zz * 4 + yy * 2 + cc

    def zrel(r):
        return (z + (r + NZ)) % NZ

    up = dev(zrel(1), y, c)
    down = dev(zrel(-1), y, c)
    side = dev(z, 1 - y, c)
    twin = dev(z, y, 1 - c)

    loads = [
        pltpu.make_async_copy(src, dst, in_sem.at[i])
        for i, (src, dst) in enumerate(
            (
                (wq_hbm.at[0], wq_ref), (cq_hbm.at[0], cq_ref), (wo_hbm.at[0], wo_ref), (co_hbm.at[0], co_ref),
                (x_hbm.at[0], x_ref), (t_hbm.at[0], t_ref), (g_hbm.at[0], g_ref),
            )
        )
    ]
    for load in loads:
        load.start()

    barrier = pltpu.get_barrier_semaphore()
    for peer in (up, down, side, twin):
        pl.semaphore_signal(barrier, inc=1, device_id={"fsdp": peer}, device_id_type=MESH)
    for k in range(1, NCKPT):
        pl.semaphore_signal(barrier, inc=1, device_id={"ckpt": (ck + k) % NCKPT}, device_id_type=MESH)

    bufs = (gq_ref, go_ref)
    pending = []

    def send(src, dst, ssem, rsem, peer):
        copy = pltpu.make_async_remote_copy(
            src_ref=src, dst_ref=dst, send_sem=ssem, recv_sem=rsem, device_id={"fsdp": peer}, device_id_type=MESH
        )
        copy.start()
        pending.append(copy)

    def landed(ref, sem):
        pltpu.make_async_copy(ref, ref, sem).wait()

    def part(ph, r, yy, cc, first, count):
        return bufs[ph].at[dev(zrel(r), yy, cc), pl.ds(first, count), :]

    def whole(ph, r, yy, cc):
        return bufs[ph].at[dev(zrel(r), yy, cc)]

    def owner_y(kind):
        return 1 - y if kind == "X" else y

    def hop_rows(piece, way, s):
        kind, first, count, last_up, last_down = piece
        if s < 3:
            return (first, count)
        return last_up if way == 0 else last_down

    def ring_send(ph, pi, way, s):
        piece = PIECES[ph][pi]
        span = hop_rows(piece, way, s)
        if span is None:
            return
        r = -s if way == 0 else s
        ref = part(ph, r, owner_y(piece[0]), c, *span)
        send(ref, ref, ring_s.at[ph, way, s, pi], ring_r.at[ph, way, s, pi], up if way == 0 else down)

    def ring_wait(ph, pi, way, s):
        piece = PIECES[ph][pi]
        span = hop_rows(piece, way, s)
        if span is None:
            return
        r = -(s + 1) if way == 0 else s + 1
        landed(part(ph, r, owner_y(piece[0]), c, *span), ring_r.at[ph, way, s, pi])

    def y_send(ph, pi, r):
        _, first, count, _, _ = PIECES[ph][pi]
        slot = 8 if pi == 1 else r % NZ
        ref = part(ph, r, y, c, first, count)
        send(ref, ref, y_s.at[ph, slot], y_r.at[ph, slot], side)

    def y_wait(ph, pi, r):
        _, first, count, _, _ = PIECES[ph][pi]
        slot = 8 if pi == 1 else r % NZ
        landed(part(ph, r, 1 - y, c, first, count), y_r.at[ph, slot])

    def twin_send(ph, r, other):
        ref = whole(ph, r, 1 - y if other else y, c)
        send(ref, ref, sib_s.at[ph, r % NZ, other], sib_r.at[ph, r % NZ, other], twin)

    def twin_wait(ph, r):
        for other in (0, 1):
            landed(whole(ph, r, 1 - y if other else y, 1 - c), sib_r.at[ph, r % NZ, other])

    def begin(ph):
        y_send(ph, 1, 0)
        for pi in (0, 1):
            for way in (0, 1):
                ring_send(ph, pi, way, 0)
        y_send(ph, 0, 0)
        twin_send(ph, 0, 0)
        y_wait(ph, 1, 0)
        for way in (0, 1):
            ring_send(ph, 2, way, 0)

    def finish_own(ph):
        y_wait(ph, 0, 0)
        twin_send(ph, 0, 1)

    def hop(ph, s):
        rels = (-(s + 1), s + 1)
        for pi in range(3):
            for way in (0, 1):
                ring_wait(ph, pi, way, s)
                if s < 3:
                    ring_send(ph, pi, way, s + 1)
                    if pi == 0:
                        y_send(ph, 0, rels[way])
                    if pi == 1:
                        twin_send(ph, rels[way], 0)
            if s == 3 and pi == 0:
                y_send(ph, 0, 4)
            if s == 3 and pi == 1:
                twin_send(ph, 4, 0)
        for r in rels if s < 3 else (4,):
            y_wait(ph, 0, r)
            twin_send(ph, r, 1)

    def project_rel(r):
        twin_wait(0, r)
        project(zrel(r), gq_ref, lt_ref, ltt_ref, p_ref, dp_ref)

    for load in loads[:4]:
        load.wait()
    gq_ref[me] = jnp.concatenate([wq_ref[...].astype(F32), cq_ref[...].astype(F32)], axis=0).astype(BF16)
    go_ref[me] = jnp.concatenate([wo_ref[...].astype(F32), co_ref[...].astype(F32)], axis=0).astype(BF16)
    pl.semaphore_wait(barrier, 4 + NCKPT - 1)
    begin(0)

    for load in loads[4:]:
        load.wait()
    normalize(x_ref, t_ref, g_ref, gain_ref, cost_ref, lt_ref, ltt_ref, gt_ref, res_ref)

    finish_own(0)
    hop(0, 0)
    project_rel(0)
    hop(0, 1)
    project_rel(-1)
    project_rel(1)
    hop(0, 2)
    begin(1)
    project_rel(-2)
    project_rel(2)
    hop(0, 3)
    finish_own(1)
    project_rel(-3)
    hop(1, 0)
    project_rel(3)
    project_rel(4)
    for s in range(1, 4):
        hop(1, s)
        lax.fori_loop(
            (s - 1) * 4, s * 4, lambda h, carry: (attend_head(h, p_ref, dp_ref, at_ref, dat_ref), carry)[1], 0
        )
    for r in range(NZ):
        twin_wait(1, r)
    mine_ref[...] = out_scores(go_ref, at_ref, dat_ref, gt_ref) + res_ref[...]

    copies = []
    for k in range(1, NCKPT):
        copy = pltpu.make_async_remote_copy(
            src_ref=mine_ref, dst_ref=sums_ref.at[k], send_sem=sum_s.at[k], recv_sem=sum_r.at[k],
            device_id={"ckpt": (ck + k) % NCKPT}, device_id_type=MESH,
        )
        copy.start()
        copies.append(copy)
    for copy in pending:
        copy.wait_send()
    total = mine_ref[...]
    for k, copy in enumerate(copies):
        copy.wait_recv()
        total = total + sums_ref[k + 1]
    out_ref[...] = total
    for copy in copies:
        copy.wait_send()


def per_device(states, state_tangent, loss_grad, norm_gain, gain_costate, qkv_weight, qkv_costate, out_weight, out_costate):
    anywhere = pl.BlockSpec(memory_space=pl.ANY)
    vmem = pl.BlockSpec(memory_space=pltpu.VMEM)
    out = pl.pallas_call(
        kernel,
        out_shape=jax.ShapeDtypeStruct((1, SEQ), F32),
        in_specs=[anywhere] * 3 + [vmem] * 2 + [anywhere] * 4,
        out_specs=vmem,
        scratch_shapes=[
            pltpu.VMEM((SEQ, D), BF16),
            pltpu.VMEM((SEQ, D), BF16),
            pltpu.VMEM((SEQ, D), BF16),
            pltpu.VMEM((72, D), BF16),
            pltpu.VMEM((72, D), BF16),
            pltpu.VMEM((24, D), BF16),
            pltpu.VMEM((24, D), BF16),
            pltpu.VMEM((NDEV, RQ, D), BF16),
            pltpu.VMEM((NDEV, RO, D), BF16),
            pltpu.VMEM((D, SEQ), BF16),
            pltpu.VMEM((D, SEQ), BF16),
            pltpu.VMEM((D, SEQ), F32),
            pltpu.VMEM((1, SEQ), F32),
            pltpu.VMEM((3 * D, SEQ), BF16),
            pltpu.VMEM((3 * D, SEQ), BF16),
            pltpu.VMEM((D, SEQ), BF16),
            pltpu.VMEM((D, SEQ), BF16),
            pltpu.VMEM((1, SEQ), F32),
            pltpu.VMEM((NCKPT, 1, SEQ), F32),
            pltpu.SemaphoreType.DMA((7,)),
            pltpu.SemaphoreType.DMA((2, 2, 4, 3)),
            pltpu.SemaphoreType.DMA((2, 2, 4, 3)),
            pltpu.SemaphoreType.DMA((2, 9)),
            pltpu.SemaphoreType.DMA((2, 9)),
            pltpu.SemaphoreType.DMA((2, NZ, 2)),
            pltpu.SemaphoreType.DMA((2, NZ, 2)),
            pltpu.SemaphoreType.DMA((NCKPT,)),
            pltpu.SemaphoreType.DMA((NCKPT,)),
        ],
        compiler_params=pltpu.CompilerParams(
            collective_id=0, has_side_effects=True, vmem_limit_bytes=48 * 1024 * 1024
        ),
        cost_estimate=pl.CostEstimate(flops=9_000_000_000, bytes_accessed=3_000_000, transcendentals=3_200_000),
        name="scores",
    )(states, state_tangent, loss_grad, norm_gain, gain_costate, qkv_weight, qkv_costate, out_weight, out_costate)
    return out.reshape(SEQ)


def solution(mesh):
    return jax.shard_map(
        per_device,
        mesh=mesh,
        in_specs=(
            P("ckpt", "fsdp", None),
            P("ckpt", "fsdp", None),
            P("ckpt", "fsdp", None),
            P("ckpt", None),
            P("ckpt", None),
            P("ckpt", "fsdp", None),
            P("ckpt", "fsdp", None),
            P("ckpt", "fsdp", None),
            P("ckpt", "fsdp", None),
        ),
        out_specs=P("fsdp"),
        check_vma=False,
    )
```

```python
import functools
import math

import jax
import jax.numpy as jnp
from jax import lax
from jax.experimental import pallas as pl
from jax.experimental.pallas import tpu as pltpu
from jax.sharding import PartitionSpec as P

D = 768
HEADS = 12
HD = 64
SEQ = 512
EPSILON = 1e-05
NEGATIVE = -1e30
BF16 = jnp.bfloat16
F32 = jnp.float32
MESH = pl.DeviceIdType.MESH
NZ = 8
NCKPT = 8
NDEV = 32
RQ = 144
RO = 48

PIECES = (
    (("B", 64, 80, (64, 48), (112, 32)), ("A", 0, 64, (0, 32), (32, 32)), ("X", 0, 64, (0, 32), (32, 32))),
    (("B", 16, 32, (16, 16), (32, 16)), ("A", 0, 16, (0, 16), None), ("X", 0, 16, None, (0, 16))),
)


def remote(src, dst, ssem, rsem, where, tag):
    copy = pltpu.make_async_remote_copy(
        src_ref=src, dst_ref=dst, send_sem=ssem, recv_sem=rsem, device_id=where, device_id_type=MESH
    )
    copy.start()
    return copy


def landed(ref, sem, tag):
    pltpu.make_async_copy(ref, ref, sem).wait()


def dot(a, b):
    return lax.dot_general(a, b, (((1,), (0,)), ((), ())), preferred_element_type=F32)


def normalize(x_ref, t_ref, g_ref, gain_ref, cost_ref, lt_ref, ltt_ref, gt_ref, res_ref):
    gain = gain_ref[...].astype(F32)
    cost = cost_ref[...].astype(F32)

    def body(i, carry):
        rows = pl.ds(pl.multiple_of(i * 128, 128), 128)
        x = x_ref[rows, :].astype(F32)
        t = t_ref[rows, :].astype(F32)
        g = g_ref[rows, :].astype(F32)
        inv = lax.rsqrt(jnp.mean(x * x, axis=1, keepdims=True) + EPSILON)
        normed = x * inv
        cross = jnp.mean(x * t, axis=1, keepdims=True)
        normed_t = t * inv - x * (inv * inv * inv) * cross
        lifted = (gain * normed).astype(BF16)
        lifted_t = (cost * normed + gain * normed_t).astype(BF16)
        lt_ref[:, rows] = lifted.T
        ltt_ref[:, rows] = lifted_t.T
        gt_ref[:, rows] = g.T
        p = g * t
        q = p[:, 0:128]
        for k in range(1, D // 128):
            q = q + p[:, 128 * k : 128 * k + 128]
        res_ref[:, rows] = jnp.sum(q.T, axis=0, keepdims=True)
        return carry

    lax.fori_loop(0, SEQ // 128, body, 0)


def project(zc, gq_ref, lt_ref, ltt_ref, p_ref, dp_ref):
    devs = pl.ds(zc * 4, 4)
    r1 = dot(gq_ref[devs].reshape(4 * RQ, D), lt_ref[...]).reshape(4, RQ, SEQ)
    r2 = dot(gq_ref[devs, 0:80, :].reshape(320, D), ltt_ref[...]).reshape(4, 80, SEQ)
    rows = pl.ds(pl.multiple_of(zc * 288, 288), 288)
    p_ref[rows, :] = r1[:, 0:72].reshape(288, SEQ).astype(BF16)
    dp_ref[rows, :] = (r2[:, 0:72] + r1[:, 72:144]).reshape(288, SEQ).astype(BF16)


def attend_head(h, p_ref, dp_ref, at_ref, dat_ref):
    def rows(base):
        return pl.ds(pl.multiple_of(base + h * HD, HD), HD)

    q, dq = p_ref[rows(0), :], dp_ref[rows(0), :]
    k, dk = p_ref[rows(D), :], dp_ref[rows(D), :]
    v, dv = p_ref[rows(2 * D), :], dp_ref[rows(2 * D), :]
    kd = jnp.concatenate([k, dk], axis=0).T
    rhs_s = jnp.concatenate([q, jnp.zeros_like(q)], axis=0)
    rhs_d = jnp.concatenate([dq, q], axis=0)
    vv = jnp.concatenate([v, dv], axis=0)
    scale2 = math.log2(math.e) / math.sqrt(HD)
    for b in range(2):
        cols = slice(256 * b, 256 * b + 256)
        jm = 256 * (b + 1)
        s = dot(kd[:jm], rhs_s[:, cols])
        d = dot(kd[:jm], rhs_d[:, cols])
        row = lax.broadcasted_iota(jnp.int32, (256, 256), 0)
        col = lax.broadcasted_iota(jnp.int32, (256, 256), 1)
        diag = jnp.where(row <= col, s[jm - 256 :], NEGATIVE)
        s = diag if b == 0 else jnp.concatenate([s[: jm - 256], diag], axis=0)
        m = jnp.max(s, axis=0, keepdims=True)
        e = jnp.exp2((s - m) * scale2)
        r = 1.0 / jnp.sum(e, axis=0, keepdims=True)
        t = jnp.sum(e * d, axis=0, keepdims=True) * r
        a = (e * r).astype(BF16)
        da = ((e * (r * (1.0 / math.sqrt(HD)))) * (d - t)).astype(BF16)
        o1 = dot(vv[:, :jm], a)
        o2 = dot(v[:, :jm], da)
        at_ref[rows(0), cols] = o1[:HD].astype(BF16)
        dat_ref[rows(0), cols] = (o1[HD:] + o2).astype(BF16)


def out_scores(go_ref, at_ref, dat_ref, gt_ref):
    total = jnp.zeros((1, SEQ), F32)
    for b in range(2):
        devs = slice(16 * b, 16 * b + 16)
        r1 = dot(go_ref[devs, 0:32, :].reshape(512, D), dat_ref[...]).reshape(16, 32, SEQ)
        r2 = dot(go_ref[devs, 16:48, :].reshape(512, D), at_ref[...]).reshape(16, 32, SEQ)
        po = (r1[:, 0:24] + r2[:, 8:32]).reshape(384, SEQ)
        total = total + jnp.sum(po * gt_ref[384 * b : 384 * b + 384, :], axis=0, keepdims=True)
    return total


def kernel(
    x_hbm, t_hbm, g_hbm, gain_hbm, cost_hbm, wq_hbm, cq_hbm, wo_hbm, co_hbm,
    out_ref,
    x_ref, t_ref, g_ref, gain_ref, cost_ref, wq_ref, cq_ref, wo_ref, co_ref,
    gq_ref, go_ref, lt_ref, ltt_ref, gt_ref, res_ref, p_ref, dp_ref, at_ref, dat_ref,
    mine_ref, sums_ref,
    in_sem, ring_s, ring_r, y_s, y_r, sib_s, sib_r, sum_s, sum_r,
):
    ck = lax.axis_index("ckpt")
    me = lax.axis_index("fsdp")
    z = me // 4
    y = (me // 2) % 2
    c = me % 2

    def dev(zz, yy, cc):
        return zz * 4 + yy * 2 + cc

    def zrel(r):
        return (z + (r + NZ)) % NZ

    up = dev(zrel(1), y, c)
    down = dev(zrel(-1), y, c)
    side = dev(z, 1 - y, c)
    twin = dev(z, y, 1 - c)

    loads = [
        pltpu.make_async_copy(src, dst, in_sem.at[i])
        for i, (src, dst) in enumerate(
            (
                (wq_hbm.at[0], wq_ref), (cq_hbm.at[0], cq_ref), (wo_hbm.at[0], wo_ref), (co_hbm.at[0], co_ref),
                (x_hbm.at[0], x_ref), (t_hbm.at[0], t_ref), (gain_hbm, gain_ref), (cost_hbm, cost_ref),
                (g_hbm.at[0], g_ref),
            )
        )
    ]
    for load in loads:
        load.start()

    barrier = pltpu.get_barrier_semaphore()
    for peer in (up, down, side, twin):
        pl.semaphore_signal(barrier, inc=1, device_id={"fsdp": peer}, device_id_type=MESH)
    for k in range(1, NCKPT):
        pl.semaphore_signal(barrier, inc=1, device_id={"ckpt": (ck + k) % NCKPT}, device_id_type=MESH)

    bufs = (gq_ref, go_ref)
    pending = []

    def send(src, dst, ssem, rsem, peer, tag):
        pending.append(remote(src, dst, ssem, rsem, {"fsdp": peer}, tag))

    def part(ph, r, yy, cc, first, count):
        return bufs[ph].at[dev(zrel(r), yy, cc), pl.ds(first, count), :]

    def whole(ph, r, yy, cc):
        return bufs[ph].at[dev(zrel(r), yy, cc)]

    def owner_y(kind):
        return 1 - y if kind == "X" else y

    def hop_rows(piece, way, s):
        kind, first, count, last_up, last_down = piece
        if s < 3:
            return (first, count)
        return last_up if way == 0 else last_down

    def ring_send(ph, pi, way, s):
        piece = PIECES[ph][pi]
        span = hop_rows(piece, way, s)
        if span is None:
            return
        r = -s if way == 0 else s
        ref = part(ph, r, owner_y(piece[0]), c, *span)
        send(ref, ref, ring_s.at[ph, way, s, pi], ring_r.at[ph, way, s, pi], up if way == 0 else down, ('ring', ph))

    def ring_wait(ph, pi, way, s):
        piece = PIECES[ph][pi]
        span = hop_rows(piece, way, s)
        if span is None:
            return
        r = -(s + 1) if way == 0 else s + 1
        landed(part(ph, r, owner_y(piece[0]), c, *span), ring_r.at[ph, way, s, pi], ('ring', ph))

    def y_rows(ph, pi, r, half):
        _, first, count, last_up, last_down = PIECES[ph][pi]
        return (first, count) if half is None else (last_up, last_down)[half]

    def y_slot(pi, r, half):
        return 8 if pi == 1 else (9 if half == 1 else r % NZ)

    def y_send(ph, pi, r, half=None):
        slot = y_slot(pi, r, half)
        ref = part(ph, r, y, c, *y_rows(ph, pi, r, half))
        send(ref, ref, y_s.at[ph, slot], y_r.at[ph, slot], side, ("y", ph))

    def y_wait(ph, pi, r, half=None):
        landed(part(ph, r, 1 - y, c, *y_rows(ph, pi, r, half)), y_r.at[ph, y_slot(pi, r, half)], ("y", ph))

    def twin_send(ph, r, other):
        ref = whole(ph, r, 1 - y if other else y, c)
        send(ref, ref, sib_s.at[ph, r % NZ, other], sib_r.at[ph, r % NZ, other], twin, ("twin", ph))

    def twin_wait(ph, r):
        for other in (0, 1):
            landed(whole(ph, r, 1 - y if other else y, 1 - c), sib_r.at[ph, r % NZ, other], ("twin", ph))

    def begin(ph):
        y_send(ph, 1, 0)
        for pi in (0, 1):
            for way in (0, 1):
                ring_send(ph, pi, way, 0)
        y_send(ph, 0, 0)
        twin_send(ph, 0, 0)

    def begin_other(ph):
        y_wait(ph, 1, 0)
        for way in (0, 1):
            ring_send(ph, 2, way, 0)

    def hop_b(ph, s):
        for way, r in ((0, -(s + 1)), (1, s + 1)):
            ring_wait(ph, 0, way, s)
            if s < 3:
                ring_send(ph, 0, way, s + 1)
                y_send(ph, 0, r)
            else:
                y_send(ph, 0, 4, way)

    def y_done(ph, r):
        if r == 4:
            y_wait(ph, 0, 4, 0)
            y_wait(ph, 0, 4, 1)
        else:
            y_wait(ph, 0, r)
        twin_send(ph, r, 1)

    def hop_a(ph, s):
        for way, r in ((0, -(s + 1)), (1, s + 1)):
            ring_wait(ph, 1, way, s)
            if s < 3:
                ring_send(ph, 1, way, s + 1)
                twin_send(ph, r, 0)
        if s == 3:
            twin_send(ph, 4, 0)

    def hop_x(ph, s):
        for way in (0, 1):
            ring_wait(ph, 2, way, s)
            if s < 3:
                ring_send(ph, 2, way, s + 1)

    def hop(ph, s):
        hop_b(ph, s)
        for r in ((-s, s) if s else (0,)):
            y_done(ph, r)
        hop_a(ph, s)
        hop_x(ph, s)

    def project_rel(r):
        twin_wait(0, r)
        project(zrel(r), gq_ref, lt_ref, ltt_ref, p_ref, dp_ref)

    first_head = (9 * zrel(4)) // 2

    def heads(lo, hi):
        def body(i, carry):
            attend_head((first_head + 5 + i) % HEADS, p_ref, dp_ref, at_ref, dat_ref)
            return carry

        lax.fori_loop(lo, hi, body, 0)

    for load in loads[:4]:
        load.wait()
    gq_ref[me] = jnp.concatenate([wq_ref[...].astype(F32), cq_ref[...].astype(F32)], axis=0).astype(BF16)
    go_ref[me] = jnp.concatenate([wo_ref[...].astype(F32), co_ref[...].astype(F32)], axis=0).astype(BF16)
    pl.semaphore_wait(barrier, 4 + NCKPT - 1)
    begin(0)

    for load in loads[4:]:
        load.wait()
    normalize(x_ref, t_ref, g_ref, gain_ref, cost_ref, lt_ref, ltt_ref, gt_ref, res_ref)
    begin_other(0)

    hop(0, 0)
    project_rel(0)
    hop(0, 1)
    project_rel(-1)
    project_rel(1)
    hop(0, 2)
    begin(1)
    begin_other(1)
    project_rel(-2)
    project_rel(2)
    hop_b(0, 3)
    hop_a(0, 3)
    y_done(0, -3)
    hop_x(0, 3)
    y_done(0, 3)
    project_rel(-3)
    hop(1, 0)
    y_done(0, 4)
    heads(0, 2)
    project_rel(3)
    hop(1, 1)
    heads(2, 4)
    hop(1, 2)
    heads(4, 7)
    project_rel(4)
    hop_b(1, 3)
    hop_a(1, 3)
    hop_x(1, 3)
    y_done(1, -3)
    y_done(1, 3)
    heads(7, 10)
    y_done(1, 4)
    heads(10, 12)
    for r in range(NZ):
        twin_wait(1, r if r <= 4 else r - NZ)
    mine_ref[...] = out_scores(go_ref, at_ref, dat_ref, gt_ref) + res_ref[...]

    copies = []
    for k in range(1, NCKPT):
        copies.append(remote(mine_ref, sums_ref.at[k], sum_s.at[k], sum_r.at[k], {"ckpt": (ck + k) % NCKPT}, ("sum", 0)))
    for copy in pending:
        copy.wait_send()
    total = mine_ref[...]
    for k, copy in enumerate(copies):
        copy.wait_recv()
        total = total + sums_ref[k + 1]
    out_ref[...] = total
    for copy in copies:
        copy.wait_send()


def per_device(states, state_tangent, loss_grad, norm_gain, gain_costate, qkv_weight, qkv_costate, out_weight, out_costate):
    hbm = pl.BlockSpec(memory_space=pltpu.HBM)
    vmem = pl.BlockSpec(memory_space=pltpu.VMEM)
    out = pl.pallas_call(
        kernel,
        out_shape=jax.ShapeDtypeStruct((1, SEQ), F32),
        in_specs=[hbm] * 9,
        out_specs=vmem,
        scratch_shapes=[
            pltpu.VMEM((SEQ, D), BF16),
            pltpu.VMEM((SEQ, D), BF16),
            pltpu.VMEM((SEQ, D), BF16),
            pltpu.VMEM((1, D), BF16),
            pltpu.VMEM((1, D), BF16),
            pltpu.VMEM((72, D), BF16),
            pltpu.VMEM((72, D), BF16),
            pltpu.VMEM((24, D), BF16),
            pltpu.VMEM((24, D), BF16),
            pltpu.VMEM((NDEV, RQ, D), BF16),
            pltpu.VMEM((NDEV, RO, D), BF16),
            pltpu.VMEM((D, SEQ), BF16),
            pltpu.VMEM((D, SEQ), BF16),
            pltpu.VMEM((D, SEQ), F32),
            pltpu.VMEM((1, SEQ), F32),
            pltpu.VMEM((3 * D, SEQ), BF16),
            pltpu.VMEM((3 * D, SEQ), BF16),
            pltpu.VMEM((D, SEQ), BF16),
            pltpu.VMEM((D, SEQ), BF16),
            pltpu.VMEM((1, SEQ), F32),
            pltpu.VMEM((NCKPT, 1, SEQ), F32),
            pltpu.SemaphoreType.DMA((9,)),
            pltpu.SemaphoreType.DMA((2, 2, 4, 3)),
            pltpu.SemaphoreType.DMA((2, 2, 4, 3)),
            pltpu.SemaphoreType.DMA((2, 10)),
            pltpu.SemaphoreType.DMA((2, 10)),
            pltpu.SemaphoreType.DMA((2, NZ, 2)),
            pltpu.SemaphoreType.DMA((2, NZ, 2)),
            pltpu.SemaphoreType.DMA((NCKPT,)),
            pltpu.SemaphoreType.DMA((NCKPT,)),
        ],
        compiler_params=pltpu.CompilerParams(
            collective_id=0, has_side_effects=True, vmem_limit_bytes=60 * 1024 * 1024
        ),
        cost_estimate=pl.CostEstimate(flops=9_000_000_000, bytes_accessed=3_000_000, transcendentals=3_200_000),
        name="scores",
    )(states, state_tangent, loss_grad, norm_gain, gain_costate, qkv_weight, qkv_costate, out_weight, out_costate)
    return out.reshape(SEQ)


def solution(mesh):
    return jax.shard_map(
        per_device,
        mesh=mesh,
        in_specs=(
            P("ckpt", "fsdp", None),
            P("ckpt", "fsdp", None),
            P("ckpt", "fsdp", None),
            P("ckpt", None),
            P("ckpt", None),
            P("ckpt", "fsdp", None),
            P("ckpt", "fsdp", None),
            P("ckpt", "fsdp", None),
            P("ckpt", "fsdp", None),
        ),
        out_specs=P("fsdp"),
        check_vma=False,
    )
```

```python
import functools
import math

import jax
import jax.numpy as jnp
from jax import lax
from jax.experimental import pallas as pl
from jax.experimental.pallas import tpu as pltpu
from jax.sharding import PartitionSpec as P

D = 768
HEADS = 12
HD = 64
SEQ = 512
EPSILON = 1e-05
NEGATIVE = -1e30
BF16 = jnp.bfloat16
F32 = jnp.float32
MESH = pl.DeviceIdType.MESH
NZ = 8
NCKPT = 8
NDEV = 32
RQ = 144
RO = 48

PIECES = (
    (("B", 64, 80, (64, 48), (112, 32)), ("A", 0, 64, (0, 32), (32, 32)), ("X", 0, 64, (0, 32), (32, 32))),
    (("B", 16, 32, (16, 16), (32, 16)), ("A", 0, 16, (0, 16), None), ("X", 0, 16, None, (0, 16))),
)


GROUPS = (2, 5, 5)
ORDER = (
    "b0", "x0", "b1", "B00d", "B00u", "A00d", "x1", "X00u", "B10d", "N", "B01u", "Y0_0",
    "X00d", "X01u", "A10d", "B01d", "Y0_-1", "Y0_-2", "A00u", "B10u", "P0", "B11d", "B02u", "X10d",
    "Y0_1", "A01d", "A10u", "B02d", "Y1_0", "A01u", "X10u", "P1", "B11u", "X01d", "A11d", "Y0_2",
    "P-2", "Y1_-1", "P-1", "B03u", "X02u", "X11d", "Y0_-3", "B12d", "Y1_1", "Y1_2", "P2", "A11u",
    "A02d", "A02u", "X02d", "B03d", "X11u", "Y0_3", "B12u", "P-3", "X12d", "H0", "Y1_3", "Y1_-2",
    "P3", "X03d", "A03u", "A12d", "X03u", "A03d", "B13d", "X12u", "Y0_4", "X13u", "A12u", "T0",
    "B13u", "H1", "X13d", "Y1_4", "P4", "Y1_-3", "A13u", "A13d", "T1", "H2",
)


def remote(src, dst, ssem, rsem, where, tag):
    copy = pltpu.make_async_remote_copy(
        src_ref=src, dst_ref=dst, send_sem=ssem, recv_sem=rsem, device_id=where, device_id_type=MESH
    )
    copy.start()
    return copy


def landed(ref, sem, tag):
    pltpu.make_async_copy(ref, ref, sem).wait()


def dot(a, b):
    return lax.dot_general(a, b, (((1,), (0,)), ((), ())), preferred_element_type=F32)


def normalize(x_ref, t_ref, g_ref, gain_ref, cost_ref, lt_ref, ltt_ref, gt_ref, res_ref):
    gain = gain_ref[...].astype(F32)
    cost = cost_ref[...].astype(F32)

    def body(i, carry):
        rows = pl.ds(pl.multiple_of(i * 128, 128), 128)
        x = x_ref[rows, :].astype(F32)
        t = t_ref[rows, :].astype(F32)
        g = g_ref[rows, :].astype(F32)
        inv = lax.rsqrt(jnp.mean(x * x, axis=1, keepdims=True) + EPSILON)
        normed = x * inv
        cross = jnp.mean(x * t, axis=1, keepdims=True)
        normed_t = t * inv - x * (inv * inv * inv) * cross
        lifted = (gain * normed).astype(BF16)
        lifted_t = (cost * normed + gain * normed_t).astype(BF16)
        lt_ref[:, rows] = lifted.T
        ltt_ref[:, rows] = lifted_t.T
        gt_ref[:, rows] = g.T
        p = g * t
        q = p[:, 0:128]
        for k in range(1, D // 128):
            q = q + p[:, 128 * k : 128 * k + 128]
        res_ref[:, rows] = jnp.sum(q.T, axis=0, keepdims=True)
        return carry

    lax.fori_loop(0, SEQ // 128, body, 0)


def project(zc, gq_ref, lt_ref, ltt_ref, p_ref, dp_ref):
    devs = pl.ds(zc * 4, 4)
    r1 = dot(gq_ref[devs].reshape(4 * RQ, D), lt_ref[...]).reshape(4, RQ, SEQ)
    r2 = dot(gq_ref[devs, 0:80, :].reshape(320, D), ltt_ref[...]).reshape(4, 80, SEQ)
    rows = pl.ds(pl.multiple_of(zc * 288, 288), 288)
    p_ref[rows, :] = r1[:, 0:72].reshape(288, SEQ).astype(BF16)
    dp_ref[rows, :] = (r2[:, 0:72] + r1[:, 72:144]).reshape(288, SEQ).astype(BF16)


def head_operands(h, p_ref, dp_ref):
    def rows(base):
        return pl.ds(pl.multiple_of(base + h * HD, HD), HD)

    q, dq = p_ref[rows(0), :], dp_ref[rows(0), :]
    k, dk = p_ref[rows(D), :], dp_ref[rows(D), :]
    v, dv = p_ref[rows(2 * D), :], dp_ref[rows(2 * D), :]
    kd = jnp.concatenate([k, dk], axis=0).T
    scale = BF16(1.0 / math.sqrt(HD))
    q, dq = q * scale, dq * scale
    rhs_s = jnp.concatenate([q, jnp.zeros_like(q)], axis=0)
    rhs_d = jnp.concatenate([dq, q], axis=0)
    return rows(0), kd, rhs_s, rhs_d, v, jnp.concatenate([v, dv], axis=0)


def softmax_block(s, d, upper):
    n = s.shape[0]
    diag = jnp.where(upper, s[n - 128 :], NEGATIVE)
    s = diag if n == 128 else jnp.concatenate([s[: n - 128], diag], axis=0)
    m = jnp.max(s, axis=0, keepdims=True)
    e = jnp.exp2((s - m) * math.log2(math.e))
    a = e * (1.0 / jnp.sum(e, axis=0, keepdims=True))
    t = jnp.sum(a * d, axis=0, keepdims=True)
    return a.astype(BF16), (a * (d - t)).astype(BF16)


def attend_heads(hs, p_ref, dp_ref, at_ref, dat_ref):
    row = lax.broadcasted_iota(jnp.int32, (128, 128), 0)
    col = lax.broadcasted_iota(jnp.int32, (128, 128), 1)
    upper = row <= col
    operands = [head_operands(h, p_ref, dp_ref) for h in hs]
    empty = jnp.zeros((128, 128), BF16)
    for b in (1, 0):
        cols = slice(256 * b, 256 * b + 256)
        n = 256 * (b + 1)
        logits = [(dot(kd[:n], rs[:, cols]), dot(kd[:n], rd[:, cols])) for _, kd, rs, rd, _, _ in operands]
        weights = []
        for s, d in logits:
            left = softmax_block(s[: n - 128, :128], d[: n - 128, :128], upper)
            right = softmax_block(s[:, 128:], d[:, 128:], upper)
            weights.append(
                [jnp.concatenate([jnp.concatenate([l, empty], axis=0), r], axis=1) for l, r in zip(left, right)]
            )
        for (rows, _, _, _, v, vv), (a, da) in zip(operands, weights):
            o1 = dot(vv[:, :n], a)
            o2 = dot(v[:, :n], da)
            at_ref[rows, cols] = o1[:HD].astype(BF16)
            dat_ref[rows, cols] = (o1[HD:] + o2).astype(BF16)


def out_scores(go_ref, at_ref, dat_ref, gt_ref):
    total = jnp.zeros((1, SEQ), F32)
    for b in range(2):
        devs = slice(16 * b, 16 * b + 16)
        r1 = dot(go_ref[devs, 0:32, :].reshape(512, D), dat_ref[...]).reshape(16, 32, SEQ)
        r2 = dot(go_ref[devs, 16:48, :].reshape(512, D), at_ref[...]).reshape(16, 32, SEQ)
        po = (r1[:, 0:24] + r2[:, 8:32]).reshape(384, SEQ)
        total = total + jnp.sum(po * gt_ref[384 * b : 384 * b + 384, :], axis=0, keepdims=True)
    return total


def kernel(
    x_hbm, t_hbm, g_hbm, gain_hbm, cost_hbm, wq_hbm, cq_hbm, wo_hbm, co_hbm,
    out_ref,
    x_ref, t_ref, g_ref, gain_ref, cost_ref, wq_ref, cq_ref, wo_ref, co_ref,
    gq_ref, go_ref, lt_ref, ltt_ref, gt_ref, res_ref, p_ref, dp_ref, at_ref, dat_ref,
    mine_ref, sums_ref,
    in_sem, ring_s, ring_r, y_s, y_r, sib_s, sib_r, sum_s, sum_r,
):
    ck = lax.axis_index("ckpt")
    me = lax.axis_index("fsdp")
    z = me // 4
    y = (me // 2) % 2
    c = me % 2

    def dev(zz, yy, cc):
        return zz * 4 + yy * 2 + cc

    def zrel(r):
        return (z + (r + NZ)) % NZ

    up = dev(zrel(1), y, c)
    down = dev(zrel(-1), y, c)
    side = dev(z, 1 - y, c)
    twin = dev(z, y, 1 - c)

    loads = [
        pltpu.make_async_copy(src, dst, in_sem.at[i])
        for i, (src, dst) in enumerate(
            (
                (wq_hbm.at[0], wq_ref), (cq_hbm.at[0], cq_ref), (wo_hbm.at[0], wo_ref), (co_hbm.at[0], co_ref),
                (x_hbm.at[0], x_ref), (t_hbm.at[0], t_ref), (gain_hbm, gain_ref), (cost_hbm, cost_ref),
                (g_hbm.at[0], g_ref),
            )
        )
    ]
    for load in loads:
        load.start()

    barrier = pltpu.get_barrier_semaphore()
    for peer in (up, down, side, twin):
        pl.semaphore_signal(barrier, inc=1, device_id={"fsdp": peer}, device_id_type=MESH)
    for k in range(1, NCKPT):
        pl.semaphore_signal(barrier, inc=1, device_id={"ckpt": (ck + k) % NCKPT}, device_id_type=MESH)

    bufs = (gq_ref, go_ref)
    pending = []

    def send(src, dst, ssem, rsem, peer, tag):
        pending.append(remote(src, dst, ssem, rsem, {"fsdp": peer}, tag))

    def part(ph, r, yy, cc, first, count):
        return bufs[ph].at[dev(zrel(r), yy, cc), pl.ds(first, count), :]

    def whole(ph, r, yy, cc):
        return bufs[ph].at[dev(zrel(r), yy, cc)]

    def owner_y(kind):
        return 1 - y if kind == "X" else y

    def hop_rows(piece, way, s):
        kind, first, count, last_up, last_down = piece
        if s < 3:
            return (first, count)
        return last_up if way == 0 else last_down

    def ring_send(ph, pi, way, s):
        piece = PIECES[ph][pi]
        span = hop_rows(piece, way, s)
        if span is None:
            return
        r = -s if way == 0 else s
        ref = part(ph, r, owner_y(piece[0]), c, *span)
        send(ref, ref, ring_s.at[ph, way, s, pi], ring_r.at[ph, way, s, pi], up if way == 0 else down, ("ring", ph, pi, way, s))

    def ring_wait(ph, pi, way, s):
        piece = PIECES[ph][pi]
        span = hop_rows(piece, way, s)
        if span is None:
            return
        r = -(s + 1) if way == 0 else s + 1
        landed(part(ph, r, owner_y(piece[0]), c, *span), ring_r.at[ph, way, s, pi], ("ring", ph, pi, way, s))

    def y_rows(ph, pi, r, half):
        _, first, count, last_up, last_down = PIECES[ph][pi]
        return (first, count) if half is None else (last_up, last_down)[half]

    def y_slot(pi, r, half):
        return 8 if pi == 1 else (9 if half == 1 else r % NZ)

    def y_send(ph, pi, r, half=None):
        slot = y_slot(pi, r, half)
        ref = part(ph, r, y, c, *y_rows(ph, pi, r, half))
        send(ref, ref, y_s.at[ph, slot], y_r.at[ph, slot], side, ("y", ph, slot))

    def y_wait(ph, pi, r, half=None):
        landed(part(ph, r, 1 - y, c, *y_rows(ph, pi, r, half)), y_r.at[ph, y_slot(pi, r, half)], ("y", ph, y_slot(pi, r, half)))

    def twin_send(ph, r, other):
        ref = whole(ph, r, 1 - y if other else y, c)
        send(ref, ref, sib_s.at[ph, r % NZ, other], sib_r.at[ph, r % NZ, other], twin, ("twin", ph, r % NZ, other))

    def twin_wait(ph, r):
        for other in (0, 1):
            landed(whole(ph, r, 1 - y if other else y, 1 - c), sib_r.at[ph, r % NZ, other], ("twin", ph, r % NZ, other))

    def begin(ph):
        y_send(ph, 1, 0)
        for pi in (0, 1):
            for way in (0, 1):
                ring_send(ph, pi, way, 0)
        y_send(ph, 0, 0)
        twin_send(ph, 0, 0)

    def begin_other(ph):
        y_wait(ph, 1, 0)
        for way in (0, 1):
            ring_send(ph, 2, way, 0)

    def ring_step(ph, pi, s, way):
        ring_wait(ph, pi, way, s)
        r = -(s + 1) if way == 0 else s + 1
        if s < 3:
            ring_send(ph, pi, way, s + 1)
            if pi == 0:
                y_send(ph, 0, r)
            if pi == 1:
                twin_send(ph, r, 0)
        elif pi == 0:
            y_send(ph, 0, 4, way)

    def y_done(ph, r):
        if r == 4:
            y_wait(ph, 0, 4, 0)
            y_wait(ph, 0, 4, 1)
        else:
            y_wait(ph, 0, r)
        twin_send(ph, r, 1)

    def project_rel(r):
        twin_wait(0, r)
        project(zrel(r), gq_ref, lt_ref, ltt_ref, p_ref, dp_ref)

    first_head = (9 * zrel(4)) // 2

    def head_group(k):
        first = first_head + 5 + sum(GROUPS[:k])
        attend_heads([(first + j) % HEADS for j in range(GROUPS[k])], p_ref, dp_ref, at_ref, dat_ref)

    def load_rest():
        for load in loads[4:]:
            load.wait()
        normalize(x_ref, t_ref, g_ref, gain_ref, cost_ref, lt_ref, ltt_ref, gt_ref, res_ref)

    def run(op):
        kind = op[0]
        if kind in "BAX":
            ring_step(int(op[1]), "BAX".index(kind), int(op[2]), "ud".index(op[3]))
        elif kind == "b":
            begin(int(op[1]))
        elif kind == "x":
            begin_other(int(op[1]))
        elif kind == "Y":
            y_done(int(op[1]), int(op[3:]))
        elif kind == "T":
            twin_send(int(op[1]), 4, 0)
        elif kind == "P":
            project_rel(int(op[1:]))
        elif kind == "H":
            head_group(int(op[1:]))
        elif kind == "N":
            load_rest()

    for load in loads[:4]:
        load.wait()
    gq_ref[me] = jnp.concatenate([wq_ref[...].astype(F32), cq_ref[...].astype(F32)], axis=0).astype(BF16)
    go_ref[me] = jnp.concatenate([wo_ref[...].astype(F32), co_ref[...].astype(F32)], axis=0).astype(BF16)
    pl.semaphore_wait(barrier, 4 + NCKPT - 1)
    for op in ORDER:
        run(op)
    for r in range(NZ):
        twin_wait(1, r if r <= 4 else r - NZ)
    mine_ref[...] = out_scores(go_ref, at_ref, dat_ref, gt_ref) + res_ref[...]

    copies = []
    for k in range(1, NCKPT):
        copies.append(remote(mine_ref, sums_ref.at[k], sum_s.at[k], sum_r.at[k], {"ckpt": (ck + k) % NCKPT}, ("sum", 0, 0)))
    for copy in pending:
        copy.wait_send()
    total = mine_ref[...]
    for k, copy in enumerate(copies):
        copy.wait_recv()
        total = total + sums_ref[k + 1]
    out_ref[...] = total
    for copy in copies:
        copy.wait_send()


def per_device(states, state_tangent, loss_grad, norm_gain, gain_costate, qkv_weight, qkv_costate, out_weight, out_costate):
    hbm = pl.BlockSpec(memory_space=pltpu.HBM)
    vmem = pl.BlockSpec(memory_space=pltpu.VMEM)
    out = pl.pallas_call(
        kernel,
        out_shape=jax.ShapeDtypeStruct((1, SEQ), F32),
        in_specs=[hbm] * 9,
        out_specs=vmem,
        scratch_shapes=[
            pltpu.VMEM((SEQ, D), BF16),
            pltpu.VMEM((SEQ, D), BF16),
            pltpu.VMEM((SEQ, D), BF16),
            pltpu.VMEM((1, D), BF16),
            pltpu.VMEM((1, D), BF16),
            pltpu.VMEM((72, D), BF16),
            pltpu.VMEM((72, D), BF16),
            pltpu.VMEM((24, D), BF16),
            pltpu.VMEM((24, D), BF16),
            pltpu.VMEM((NDEV, RQ, D), BF16),
            pltpu.VMEM((NDEV, RO, D), BF16),
            pltpu.VMEM((D, SEQ), BF16),
            pltpu.VMEM((D, SEQ), BF16),
            pltpu.VMEM((D, SEQ), F32),
            pltpu.VMEM((1, SEQ), F32),
            pltpu.VMEM((3 * D, SEQ), BF16),
            pltpu.VMEM((3 * D, SEQ), BF16),
            pltpu.VMEM((D, SEQ), BF16),
            pltpu.VMEM((D, SEQ), BF16),
            pltpu.VMEM((1, SEQ), F32),
            pltpu.VMEM((NCKPT, 1, SEQ), F32),
            pltpu.SemaphoreType.DMA((9,)),
            pltpu.SemaphoreType.DMA((2, 2, 4, 3)),
            pltpu.SemaphoreType.DMA((2, 2, 4, 3)),
            pltpu.SemaphoreType.DMA((2, 10)),
            pltpu.SemaphoreType.DMA((2, 10)),
            pltpu.SemaphoreType.DMA((2, NZ, 2)),
            pltpu.SemaphoreType.DMA((2, NZ, 2)),
            pltpu.SemaphoreType.DMA((NCKPT,)),
            pltpu.SemaphoreType.DMA((NCKPT,)),
        ],
        compiler_params=pltpu.CompilerParams(
            collective_id=0, has_side_effects=True, vmem_limit_bytes=60 * 1024 * 1024
        ),
        cost_estimate=pl.CostEstimate(flops=9_000_000_000, bytes_accessed=3_000_000, transcendentals=3_200_000),
        name="scores",
    )(states, state_tangent, loss_grad, norm_gain, gain_costate, qkv_weight, qkv_costate, out_weight, out_costate)
    return out.reshape(SEQ)


def solution(mesh):
    return jax.shard_map(
        per_device,
        mesh=mesh,
        in_specs=(
            P("ckpt", "fsdp", None),
            P("ckpt", "fsdp", None),
            P("ckpt", "fsdp", None),
            P("ckpt", None),
            P("ckpt", None),
            P("ckpt", "fsdp", None),
            P("ckpt", "fsdp", None),
            P("ckpt", "fsdp", None),
            P("ckpt", "fsdp", None),
        ),
        out_specs=P("fsdp"),
        check_vma=False,
    )
```

```python
import functools
import math

import jax
import jax.numpy as jnp
from jax import lax
from jax.experimental import pallas as pl
from jax.experimental.pallas import tpu as pltpu
from jax.sharding import PartitionSpec as P

D = 768
HEADS = 12
HD = 64
SEQ = 512
EPSILON = 1e-05
NEGATIVE = -1e30
BF16 = jnp.bfloat16
F32 = jnp.float32
MESH = pl.DeviceIdType.MESH
NZ = 8
NCKPT = 8
NDEV = 32
RQ = 144
RO = 48

PIECES = (
    (("B", 64, 80, (64, 48), (112, 32)), ("A", 0, 64, (0, 32), (32, 32)), ("X", 0, 64, (0, 32), (32, 32))),
    (("B", 16, 32, (16, 16), (32, 16)), ("A", 0, 16, (0, 16), None), ("X", 0, 16, None, (0, 16))),
)


GROUPS = (2, 3, 2, 5)
ORDER = (
    "b1", "b0", "N", "x1", "Y1_0", "B10d", "A10d", "x0", "B00d", "B00u", "Y0_0", "A00u",
    "A00d", "X00u", "B11d", "B01u", "X00d", "P0", "B01d", "Y0_-1", "Y0_1", "P-1", "B10u", "A11d",
    "X10d", "A01d", "A01u", "X01u", "Y0_-2", "X01d", "X10u", "Y1_1", "B02u", "Y0_2", "Y1_-1", "B02d",
    "A10u", "P2", "B11u", "B12d", "P1", "A12d", "A02u", "X02u", "Y0_-3", "P-2", "X11u", "X11d",
    "A02d", "Y1_2", "P-3", "B03u", "X02d", "Y0_3", "H0", "A11u", "B03d", "B12u", "P3", "X12d",
    "B13d", "H2", "Y1_3", "A13d", "A03d", "X03u", "Y1_-2", "X12u", "A03u", "X13u", "A12u", "X03d",
    "T0", "Y0_4", "B13u", "H1", "P4", "Y1_-3", "A13u", "T1", "X13d", "Y1_4", "H3",
)


def remote(src, dst, ssem, rsem, where, tag):
    copy = pltpu.make_async_remote_copy(
        src_ref=src, dst_ref=dst, send_sem=ssem, recv_sem=rsem, device_id=where, device_id_type=MESH
    )
    copy.start()
    return copy


def landed(ref, sem, tag):
    pltpu.make_async_copy(ref, ref, sem).wait()


def dot(a, b):
    return lax.dot_general(a, b, (((1,), (0,)), ((), ())), preferred_element_type=F32)


def normalize(x_ref, t_ref, g_ref, gain_ref, cost_ref, lt_ref, ltt_ref, gt_ref, res_ref):
    gain = gain_ref[...].astype(F32)
    cost = cost_ref[...].astype(F32)

    def body(i, carry):
        rows = pl.ds(pl.multiple_of(i * 128, 128), 128)
        x = x_ref[rows, :].astype(F32)
        t = t_ref[rows, :].astype(F32)
        g = g_ref[rows, :].astype(F32)
        inv = lax.rsqrt(jnp.mean(x * x, axis=1, keepdims=True) + EPSILON)
        normed = x * inv
        cross = jnp.mean(x * t, axis=1, keepdims=True)
        normed_t = t * inv - x * (inv * inv * inv) * cross
        lifted = (gain * normed).astype(BF16)
        lifted_t = (cost * normed + gain * normed_t).astype(BF16)
        lt_ref[:, rows] = lifted.T
        ltt_ref[:, rows] = lifted_t.T
        gt_ref[:, rows] = g.T
        p = g * t
        q = p[:, 0:128]
        for k in range(1, D // 128):
            q = q + p[:, 128 * k : 128 * k + 128]
        res_ref[:, rows] = jnp.sum(q.T, axis=0, keepdims=True)
        return carry

    lax.fori_loop(0, SEQ // 128, body, 0)


def project(zc, gq_ref, lt_ref, ltt_ref, p_ref, dp_ref):
    devs = pl.ds(zc * 4, 4)
    r1 = dot(gq_ref[devs].reshape(4 * RQ, D), lt_ref[...]).reshape(4, RQ, SEQ)
    r2 = dot(gq_ref[devs, 0:80, :].reshape(320, D), ltt_ref[...]).reshape(4, 80, SEQ)
    rows = pl.ds(pl.multiple_of(zc * 288, 288), 288)
    p_ref[rows, :] = r1[:, 0:72].reshape(288, SEQ).astype(BF16)
    dp_ref[rows, :] = (r2[:, 0:72] + r1[:, 72:144]).reshape(288, SEQ).astype(BF16)


def head_operands(h, p_ref, dp_ref):
    def rows(base):
        return pl.ds(pl.multiple_of(base + h * HD, HD), HD)

    q, dq = p_ref[rows(0), :], dp_ref[rows(0), :]
    k, dk = p_ref[rows(D), :], dp_ref[rows(D), :]
    v, dv = p_ref[rows(2 * D), :], dp_ref[rows(2 * D), :]
    kd = jnp.concatenate([k, dk], axis=0).T
    scale = BF16(1.0 / math.sqrt(HD))
    q, dq = q * scale, dq * scale
    rhs_s = jnp.concatenate([q, jnp.zeros_like(q)], axis=0)
    rhs_d = jnp.concatenate([dq, q], axis=0)
    return rows(0), kd, rhs_s, rhs_d, v, jnp.concatenate([v, dv], axis=0)


def softmax_block(s, d, upper):
    n = s.shape[0]
    diag = jnp.where(upper, s[n - 128 :], NEGATIVE)
    s = diag if n == 128 else jnp.concatenate([s[: n - 128], diag], axis=0)
    m = jnp.max(s, axis=0, keepdims=True)
    e = jnp.exp2((s - m) * math.log2(math.e))
    a = e * (1.0 / jnp.sum(e, axis=0, keepdims=True))
    t = jnp.sum(a * d, axis=0, keepdims=True)
    return a.astype(BF16), (a * (d - t)).astype(BF16)


def attend_heads(hs, p_ref, dp_ref, at_ref, dat_ref):
    row = lax.broadcasted_iota(jnp.int32, (128, 128), 0)
    col = lax.broadcasted_iota(jnp.int32, (128, 128), 1)
    upper = row <= col
    operands = [head_operands(h, p_ref, dp_ref) for h in hs]
    empty = jnp.zeros((128, 128), BF16)
    for b in (1, 0):
        cols = slice(256 * b, 256 * b + 256)
        n = 256 * (b + 1)
        logits = [(dot(kd[:n], rs[:, cols]), dot(kd[:n], rd[:, cols])) for _, kd, rs, rd, _, _ in operands]
        weights = []
        for s, d in logits:
            left = softmax_block(s[: n - 128, :128], d[: n - 128, :128], upper)
            right = softmax_block(s[:, 128:], d[:, 128:], upper)
            weights.append(
                [jnp.concatenate([jnp.concatenate([l, empty], axis=0), r], axis=1) for l, r in zip(left, right)]
            )
        for (rows, _, _, _, v, vv), (a, da) in zip(operands, weights):
            o1 = dot(vv[:, :n], a)
            o2 = dot(v[:, :n], da)
            at_ref[rows, cols] = o1[:HD].astype(BF16)
            dat_ref[rows, cols] = (o1[HD:] + o2).astype(BF16)


def out_scores(go_ref, at_ref, dat_ref, gt_ref):
    total = jnp.zeros((1, SEQ), F32)
    for b in range(2):
        devs = slice(16 * b, 16 * b + 16)
        r1 = dot(go_ref[devs, 0:32, :].reshape(512, D), dat_ref[...]).reshape(16, 32, SEQ)
        r2 = dot(go_ref[devs, 16:48, :].reshape(512, D), at_ref[...]).reshape(16, 32, SEQ)
        po = (r1[:, 0:24] + r2[:, 8:32]).reshape(384, SEQ)
        total = total + jnp.sum(po * gt_ref[384 * b : 384 * b + 384, :], axis=0, keepdims=True)
    return total


def kernel(
    x_hbm, t_hbm, g_hbm, gain_hbm, cost_hbm, wq_hbm, cq_hbm, wo_hbm, co_hbm,
    out_ref,
    x_ref, t_ref, g_ref, gain_ref, cost_ref, wq_ref, cq_ref, wo_ref, co_ref,
    gq_ref, go_ref, lt_ref, ltt_ref, gt_ref, res_ref, p_ref, dp_ref, at_ref, dat_ref,
    mine_ref, sums_ref,
    in_sem, sent, ring_r, y_r, twin_r, sum_r,
):
    ck = lax.axis_index("ckpt")
    me = lax.axis_index("fsdp")
    z = me // 4
    y = (me // 2) % 2
    c = me % 2

    def dev(zz, yy, cc):
        return zz * 4 + yy * 2 + cc

    def zrel(r):
        return (z + (r + NZ)) % NZ

    up = dev(zrel(1), y, c)
    down = dev(zrel(-1), y, c)
    side = dev(z, 1 - y, c)
    twin = dev(z, y, 1 - c)

    for i, src, dst in (
        (0, wq_hbm.at[0], wq_ref), (0, cq_hbm.at[0], cq_ref), (0, wo_hbm.at[0], wo_ref), (0, co_hbm.at[0], co_ref),
        (1, x_hbm.at[0], x_ref), (1, t_hbm.at[0], t_ref), (1, g_hbm.at[0], g_ref),
        (2, gain_hbm, gain_ref), (3, cost_hbm, cost_ref),
    ):
        pltpu.make_async_copy(src, dst, in_sem.at[i]).start()

    barrier = pltpu.get_barrier_semaphore()
    for peer in (up, down, side, twin):
        pl.semaphore_signal(barrier, inc=1, device_id={"fsdp": peer}, device_id_type=MESH)
    for k in range(1, NCKPT):
        pl.semaphore_signal(barrier, inc=1, device_id={"ckpt": (ck + k) % NCKPT}, device_id_type=MESH)

    bufs = (gq_ref, go_ref)

    def send(ref, slot, rsem, peer, tag):
        remote(ref, ref, sent.at[slot], rsem, {"fsdp": peer}, tag)

    def part(ph, r, yy, cc, first, count):
        return bufs[ph].at[dev(zrel(r), yy, cc), pl.ds(first, count), :]

    def whole(ph, r, yy, cc):
        return bufs[ph].at[dev(zrel(r), yy, cc)]

    def owner_y(kind):
        return 1 - y if kind == "X" else y

    def hop_rows(piece, way, s):
        kind, first, count, last_up, last_down = piece
        if s < 3:
            return (first, count)
        return last_up if way == 0 else last_down

    def ring_send(ph, pi, way, s):
        piece = PIECES[ph][pi]
        span = hop_rows(piece, way, s)
        if span is None:
            return
        r = -s if way == 0 else s
        ref = part(ph, r, owner_y(piece[0]), c, *span)
        send(ref, 0, ring_r.at[ph, way, s, pi], up if way == 0 else down, ("ring", ph, pi, way, s))

    def ring_wait(ph, pi, way, s):
        piece = PIECES[ph][pi]
        span = hop_rows(piece, way, s)
        if span is None:
            return
        r = -(s + 1) if way == 0 else s + 1
        landed(part(ph, r, owner_y(piece[0]), c, *span), ring_r.at[ph, way, s, pi], ("ring", ph, pi, way, s))

    def y_rows(ph, pi, r, half):
        _, first, count, last_up, last_down = PIECES[ph][pi]
        return (first, count) if half is None else (last_up, last_down)[half]

    def y_slot(pi, r):
        return 8 if pi == 1 else r % NZ

    def y_send(ph, pi, r, half=None):
        slot = y_slot(pi, r)
        ref = part(ph, r, y, c, *y_rows(ph, pi, r, half))
        send(ref, 0, y_r.at[ph, slot], side, ("y", ph, slot))

    def y_wait(ph, pi, r):
        slot = y_slot(pi, r)
        landed(part(ph, r, 1 - y, c, *y_rows(ph, pi, r, None)), y_r.at[ph, slot], ("y", ph, slot))

    def twin_send(ph, r, other):
        ref = whole(ph, r, 1 - y if other else y, c)
        send(ref, 1 + ph, twin_r.at[r % NZ if ph == 0 else NZ], twin, ("twin", ph, r % NZ, other))

    def twin_wait(r):
        landed(gq_ref.at[pl.ds(0, 2)], twin_r.at[r % NZ], ("twin", 0, r % NZ))

    def begin(ph):
        y_send(ph, 1, 0)
        for pi in (0, 1):
            for way in (0, 1):
                ring_send(ph, pi, way, 0)
        y_send(ph, 0, 0)
        twin_send(ph, 0, 0)

    def begin_other(ph):
        y_wait(ph, 1, 0)
        for way in (0, 1):
            ring_send(ph, 2, way, 0)

    def ring_step(ph, pi, s, way):
        ring_wait(ph, pi, way, s)
        r = -(s + 1) if way == 0 else s + 1
        if s < 3:
            ring_send(ph, pi, way, s + 1)
            if pi == 0:
                y_send(ph, 0, r)
            if pi == 1:
                twin_send(ph, r, 0)
        elif pi == 0:
            y_send(ph, 0, 4, way)

    def y_done(ph, r):
        y_wait(ph, 0, r)
        twin_send(ph, r, 1)

    def project_rel(r):
        twin_wait(r)
        project(zrel(r), gq_ref, lt_ref, ltt_ref, p_ref, dp_ref)

    first_head = (9 * zrel(4)) // 2

    def head_group(k):
        first = first_head + 5 + sum(GROUPS[:k])
        attend_heads([(first + j) % HEADS for j in range(GROUPS[k])], p_ref, dp_ref, at_ref, dat_ref)

    def load_rest():
        landed(go_ref, in_sem.at[1], ("in", 0))
        landed(gain_ref, in_sem.at[2], ("in", 0))
        landed(cost_ref, in_sem.at[3], ("in", 0))
        normalize(x_ref, t_ref, g_ref, gain_ref, cost_ref, lt_ref, ltt_ref, gt_ref, res_ref)

    def run(op):
        kind = op[0]
        if kind in "BAX":
            ring_step(int(op[1]), "BAX".index(kind), int(op[2]), "ud".index(op[3]))
        elif kind == "b":
            begin(int(op[1]))
        elif kind == "x":
            begin_other(int(op[1]))
        elif kind == "Y":
            y_done(int(op[1]), int(op[3:]))
        elif kind == "T":
            twin_send(int(op[1]), 4, 0)
        elif kind == "P":
            project_rel(int(op[1:]))
        elif kind == "H":
            head_group(int(op[1:]))
        elif kind == "N":
            load_rest()

    landed(x_ref.at[pl.ds(0, 192)], in_sem.at[0], ("in", 0))
    gq_ref[me] = jnp.concatenate([wq_ref[...].astype(F32), cq_ref[...].astype(F32)], axis=0).astype(BF16)
    go_ref[me] = jnp.concatenate([wo_ref[...].astype(F32), co_ref[...].astype(F32)], axis=0).astype(BF16)
    pl.semaphore_wait(barrier, 4 + NCKPT - 1)
    for op in ORDER:
        run(op)
    landed(go_ref.at[pl.ds(0, 16)], twin_r.at[NZ], ("twin", 1))
    mine_ref[...] = out_scores(go_ref, at_ref, dat_ref, gt_ref) + res_ref[...]

    for k in range(1, NCKPT):
        remote(mine_ref, sums_ref.at[k], sent.at[3], sum_r.at[k], {"ckpt": (ck + k) % NCKPT}, ("sum", 0, k))
    landed(gq_ref.at[pl.ds(0, 20)], sent.at[0], ("sent", 0))
    landed(gq_ref.at[pl.ds(0, 16)], sent.at[1], ("sent", 1))
    landed(go_ref.at[pl.ds(0, 16)], sent.at[2], ("sent", 2))
    total = mine_ref[...]
    for k in range(1, NCKPT):
        landed(sums_ref.at[k], sum_r.at[k], ("sum", 0, k))
        total = total + sums_ref[k]
    out_ref[...] = total
    landed(sums_ref.at[pl.ds(1, NCKPT - 1)], sent.at[3], ("sent", 3))


def per_device(states, state_tangent, loss_grad, norm_gain, gain_costate, qkv_weight, qkv_costate, out_weight, out_costate):
    hbm = pl.BlockSpec(memory_space=pltpu.HBM)
    vmem = pl.BlockSpec(memory_space=pltpu.VMEM)
    out = pl.pallas_call(
        kernel,
        out_shape=jax.ShapeDtypeStruct((1, SEQ), F32),
        in_specs=[hbm] * 9,
        out_specs=vmem,
        scratch_shapes=[
            pltpu.VMEM((SEQ, D), BF16),
            pltpu.VMEM((SEQ, D), BF16),
            pltpu.VMEM((SEQ, D), BF16),
            pltpu.VMEM((1, D), BF16),
            pltpu.VMEM((1, D), BF16),
            pltpu.VMEM((72, D), BF16),
            pltpu.VMEM((72, D), BF16),
            pltpu.VMEM((24, D), BF16),
            pltpu.VMEM((24, D), BF16),
            pltpu.VMEM((NDEV, RQ, D), BF16),
            pltpu.VMEM((NDEV, RO, D), BF16),
            pltpu.VMEM((D, SEQ), BF16),
            pltpu.VMEM((D, SEQ), BF16),
            pltpu.VMEM((D, SEQ), F32),
            pltpu.VMEM((1, SEQ), F32),
            pltpu.VMEM((3 * D, SEQ), BF16),
            pltpu.VMEM((3 * D, SEQ), BF16),
            pltpu.VMEM((D, SEQ), BF16),
            pltpu.VMEM((D, SEQ), BF16),
            pltpu.VMEM((1, SEQ), F32),
            pltpu.VMEM((NCKPT, 1, SEQ), F32),
            pltpu.SemaphoreType.DMA((4,)),
            pltpu.SemaphoreType.DMA((4,)),
            pltpu.SemaphoreType.DMA((2, 2, 4, 3)),
            pltpu.SemaphoreType.DMA((2, 9)),
            pltpu.SemaphoreType.DMA((NZ + 1,)),
            pltpu.SemaphoreType.DMA((NCKPT,)),
        ],
        compiler_params=pltpu.CompilerParams(
            collective_id=0, has_side_effects=True, vmem_limit_bytes=60 * 1024 * 1024
        ),
        cost_estimate=pl.CostEstimate(flops=9_000_000_000, bytes_accessed=3_000_000, transcendentals=3_200_000),
        name="scores",
    )(states, state_tangent, loss_grad, norm_gain, gain_costate, qkv_weight, qkv_costate, out_weight, out_costate)
    return out.reshape(SEQ)


def solution(mesh):
    return jax.shard_map(
        per_device,
        mesh=mesh,
        in_specs=(
            P("ckpt", "fsdp", None),
            P("ckpt", "fsdp", None),
            P("ckpt", "fsdp", None),
            P("ckpt", None),
            P("ckpt", None),
            P("ckpt", "fsdp", None),
            P("ckpt", "fsdp", None),
            P("ckpt", "fsdp", None),
            P("ckpt", "fsdp", None),
        ),
        out_specs=P("fsdp"),
        check_vma=False,
    )
```

```python
import functools
import math

import jax
import jax.numpy as jnp
from jax import lax
from jax.experimental import pallas as pl
from jax.experimental.pallas import tpu as pltpu
from jax.sharding import PartitionSpec as P

D = 768
HEADS = 12
HD = 64
SEQ = 512
EPSILON = 1e-05
NEGATIVE = -1e30
BF16 = jnp.bfloat16
F32 = jnp.float32
MESH = pl.DeviceIdType.MESH
NZ = 8
NCKPT = 8
NDEV = 32
RQ = 144
RO = 48

PIECES = (
    (("B", 64, 80, (64, 48), (112, 32)), ("A", 0, 64, (0, 32), (32, 32)), ("X", 0, 64, (0, 32), (32, 32))),
    (("B", 16, 32, (16, 16), (32, 16)), ("A", 0, 16, (0, 16), None), ("X", 0, 16, None, (0, 16))),
)


OUT_GROUPS = ((0, -1, 1), (-2, 2), (3, -3), (4,))
GROUPS = (2, 3, 2, 5)
ORDER = (
    "b1", "b0", "x1", "Y1_0", "x0", "B00u", "A00u", "B00d", "B10d", "A10d", "A00d", "Y0_0",
    "X00u", "Y0_-1", "X00d", "Y0_1", "B01u", "B01d", "N", "X10d", "B10u", "P0", "A01u", "X01u",
    "P1", "Y0_-2", "A10u", "B02u", "X01d", "Y0_2", "Y1_1", "X10u", "B02d", "A01d", "Y1_-1", "B11u",
    "P-1", "A02u", "B11d", "P2", "A11d", "X11d", "U0", "X02u", "Y0_-3", "X02d", "P-2", "A11u",
    "B03d", "P-3", "A02d", "B03u", "Y0_3", "H0", "B12d", "X11u", "A12d", "B12u", "Y1_-2", "Y1_2",
    "X12d", "P3", "H2", "A03u", "X03u", "U1", "B13d", "A12u", "A13d", "X03d", "Y0_4", "A03d",
    "T0", "X13d", "B13u", "H1", "X12u", "X13u", "Y1_3", "P4", "Y1_4", "Y1_-3", "A13u", "T1",
    "H3", "U3", "U2",
)


def remote(src, dst, ssem, rsem, where, tag):
    copy = pltpu.make_async_remote_copy(
        src_ref=src, dst_ref=dst, send_sem=ssem, recv_sem=rsem, device_id=where, device_id_type=MESH
    )
    copy.start()
    return copy


def landed(ref, sem, tag):
    pltpu.make_async_copy(ref, ref, sem).wait()


def dot(a, b):
    return lax.dot_general(a, b, (((1,), (0,)), ((), ())), preferred_element_type=F32)


def normalize(x_ref, t_ref, g_ref, gain_ref, cost_ref, lt_ref, ltt_ref, gt_ref, res_ref):
    gain = gain_ref[...].astype(F32)
    cost = cost_ref[...].astype(F32)

    def body(i, carry):
        rows = pl.ds(pl.multiple_of(i * 128, 128), 128)
        x = x_ref[rows, :].astype(F32)
        t = t_ref[rows, :].astype(F32)
        g = g_ref[rows, :].astype(F32)
        inv = lax.rsqrt(jnp.mean(x * x, axis=1, keepdims=True) + EPSILON)
        normed = x * inv
        cross = jnp.mean(x * t, axis=1, keepdims=True)
        normed_t = t * inv - x * (inv * inv * inv) * cross
        lifted = (gain * normed).astype(BF16)
        lifted_t = (cost * normed + gain * normed_t).astype(BF16)
        lt_ref[:, rows] = lifted.T
        ltt_ref[:, rows] = lifted_t.T
        gt_ref[:, rows] = g_ref[rows, :].T
        p = g * t
        q = p[:, 0:128]
        for k in range(1, D // 128):
            q = q + p[:, 128 * k : 128 * k + 128]
        res_ref[:, rows] = jnp.sum(q.T, axis=0, keepdims=True)
        return carry

    lax.fori_loop(0, SEQ // 128, body, 0)


def project(zc, gq_ref, lt_ref, ltt_ref, p_ref, dp_ref):
    devs = pl.ds(zc * 4, 4)
    r1 = dot(gq_ref[devs].reshape(4 * RQ, D), lt_ref[...]).reshape(4, RQ, SEQ)
    r2 = dot(gq_ref[devs, 0:80, :].reshape(320, D), ltt_ref[...]).reshape(4, 80, SEQ)
    rows = pl.ds(pl.multiple_of(zc * 288, 288), 288)
    p_ref[rows, :] = r1[:, 0:72].reshape(288, SEQ).astype(BF16)
    dp_ref[rows, :] = (r2[:, 0:72] + r1[:, 72:144]).reshape(288, SEQ).astype(BF16)


def head_operands(h, p_ref, dp_ref):
    def rows(base):
        return pl.ds(pl.multiple_of(base + h * HD, HD), HD)

    q, dq = p_ref[rows(0), :], dp_ref[rows(0), :]
    k, dk = p_ref[rows(D), :], dp_ref[rows(D), :]
    v, dv = p_ref[rows(2 * D), :], dp_ref[rows(2 * D), :]
    kd = jnp.concatenate([k, dk], axis=0).T
    scale = BF16(1.0 / math.sqrt(HD))
    q, dq = q * scale, dq * scale
    rhs_s = jnp.concatenate([q, jnp.zeros_like(q)], axis=0)
    rhs_d = jnp.concatenate([dq, q], axis=0)
    return rows(0), kd, rhs_s, rhs_d, v, jnp.concatenate([v, dv], axis=0)


def softmax_block(s, d, upper):
    n = s.shape[0]
    diag = jnp.where(upper, s[n - 128 :], NEGATIVE)
    s = diag if n == 128 else jnp.concatenate([s[: n - 128], diag], axis=0)
    m = jnp.max(s, axis=0, keepdims=True)
    e = jnp.exp2((s - m) * math.log2(math.e))
    a = e * (1.0 / jnp.sum(e, axis=0, keepdims=True))
    t = jnp.sum(a * d, axis=0, keepdims=True)
    return a.astype(BF16), (a * (d - t)).astype(BF16)


def attend_heads(hs, p_ref, dp_ref, at_ref, dat_ref):
    row = lax.broadcasted_iota(jnp.int32, (128, 128), 0)
    col = lax.broadcasted_iota(jnp.int32, (128, 128), 1)
    upper = row <= col
    operands = [head_operands(h, p_ref, dp_ref) for h in hs]
    empty = jnp.zeros((128, 128), BF16)
    for b in (1, 0):
        cols = slice(256 * b, 256 * b + 256)
        n = 256 * (b + 1)
        logits = [(dot(kd[:n], rs[:, cols]), dot(kd[:n], rd[:, cols])) for _, kd, rs, rd, _, _ in operands]
        weights = []
        for s, d in logits:
            left = softmax_block(s[: n - 128, :128], d[: n - 128, :128], upper)
            right = softmax_block(s[:, 128:], d[:, 128:], upper)
            weights.append(
                [jnp.concatenate([jnp.concatenate([l, empty], axis=0), r], axis=1) for l, r in zip(left, right)]
            )
        for (rows, _, _, _, v, vv), (a, da) in zip(operands, weights):
            o1 = dot(vv[:, :n], a)
            o2 = dot(v[:, :n], da)
            at_ref[rows, cols] = o1[:HD].astype(BF16)
            dat_ref[rows, cols] = (o1[HD:] + o2).astype(BF16)


def grad_times_out(zcs, first, go_ref, gt_ref, u_ref, uc_ref):
    blocks = [go_ref[pl.ds(zc * 4, 4)].astype(F32) for zc in zcs]
    grad = jnp.concatenate([gt_ref[pl.ds(pl.multiple_of(zc * 96, 96), 96), :] for zc in zcs], axis=0)
    for lo, ref in ((0, u_ref), (24, uc_ref)):
        w = jnp.concatenate([b[:, lo : lo + 24].reshape(96, D) for b in blocks], axis=0).astype(BF16)
        term = dot(w.T, grad)
        ref[...] = term if first else ref[...] + term


def out_scores(at_ref, dat_ref, u_ref, uc_ref):
    total = jnp.zeros((1, SEQ), F32)
    for i in range(0, D, 128):
        rows = slice(i, i + 128)
        term = dat_ref[rows, :].astype(F32) * u_ref[rows, :] + at_ref[rows, :].astype(F32) * uc_ref[rows, :]
        total = total + jnp.sum(term, axis=0, keepdims=True)
    return total


def kernel(
    x_hbm, t_hbm, g_hbm, gain_hbm, cost_hbm, wq_hbm, cq_hbm, wo_hbm, co_hbm,
    out_ref,
    x_ref, t_ref, g_ref, gain_ref, cost_ref, wq_ref, cq_ref, wo_ref, co_ref,
    gq_ref, go_ref, lt_ref, ltt_ref, gt_ref, res_ref, p_ref, dp_ref, at_ref, dat_ref, u_ref, uc_ref,
    mine_ref, sums_ref,
    in_sem, sent, ring_r, y_r, twin_r, sum_r,
):
    ck = lax.axis_index("ckpt")
    me = lax.axis_index("fsdp")
    z = me // 4
    y = (me // 2) % 2
    c = me % 2

    def dev(zz, yy, cc):
        return zz * 4 + yy * 2 + cc

    def zrel(r):
        return (z + (r + NZ)) % NZ

    up = dev(zrel(1), y, c)
    down = dev(zrel(-1), y, c)
    side = dev(z, 1 - y, c)
    twin = dev(z, y, 1 - c)

    barrier = pltpu.get_barrier_semaphore()
    for peer in (up, down, side, twin):
        pl.semaphore_signal(barrier, inc=1, device_id={"fsdp": peer}, device_id_type=MESH)
    for i, src, dst in (
        (0, wq_hbm.at[0], wq_ref), (0, cq_hbm.at[0], cq_ref), (4, wo_hbm.at[0], wo_ref), (4, co_hbm.at[0], co_ref),
    ):
        pltpu.make_async_copy(src, dst, in_sem.at[i]).start()
    for k in range(1, NCKPT):
        pl.semaphore_signal(barrier, inc=1, device_id={"ckpt": (ck + k) % NCKPT}, device_id_type=MESH)
    for i, src, dst in (
        (1, x_hbm.at[0], x_ref), (1, t_hbm.at[0], t_ref), (1, g_hbm.at[0], g_ref),
        (2, gain_hbm, gain_ref), (3, cost_hbm, cost_ref),
    ):
        pltpu.make_async_copy(src, dst, in_sem.at[i]).start()

    bufs = (gq_ref, go_ref)

    def send(ref, slot, rsem, peer, tag):
        remote(ref, ref, sent.at[slot], rsem, {"fsdp": peer}, tag)

    def part(ph, r, yy, cc, first, count):
        return bufs[ph].at[dev(zrel(r), yy, cc), pl.ds(first, count), :]

    def whole(ph, r, yy, cc):
        return bufs[ph].at[dev(zrel(r), yy, cc)]

    def owner_y(kind):
        return 1 - y if kind == "X" else y

    def hop_rows(piece, way, s):
        kind, first, count, last_up, last_down = piece
        if s < 3:
            return (first, count)
        return last_up if way == 0 else last_down

    def ring_send(ph, pi, way, s):
        piece = PIECES[ph][pi]
        span = hop_rows(piece, way, s)
        if span is None:
            return
        r = -s if way == 0 else s
        ref = part(ph, r, owner_y(piece[0]), c, *span)
        send(ref, 0, ring_r.at[ph, way, s, pi], up if way == 0 else down, ("ring", ph, pi, way, s))

    def ring_wait(ph, pi, way, s):
        piece = PIECES[ph][pi]
        span = hop_rows(piece, way, s)
        if span is None:
            return
        r = -(s + 1) if way == 0 else s + 1
        landed(part(ph, r, owner_y(piece[0]), c, *span), ring_r.at[ph, way, s, pi], ("ring", ph, pi, way, s))

    def y_rows(ph, pi, r, half):
        _, first, count, last_up, last_down = PIECES[ph][pi]
        return (first, count) if half is None else (last_up, last_down)[half]

    def y_slot(pi, r):
        return 8 if pi == 1 else r % NZ

    def y_send(ph, pi, r, half=None):
        slot = y_slot(pi, r)
        ref = part(ph, r, y, c, *y_rows(ph, pi, r, half))
        send(ref, 0, y_r.at[ph, slot], side, ("y", ph, slot))

    def y_wait(ph, pi, r):
        slot = y_slot(pi, r)
        landed(part(ph, r, 1 - y, c, *y_rows(ph, pi, r, None)), y_r.at[ph, slot], ("y", ph, slot))

    def twin_send(ph, r, other):
        ref = whole(ph, r, 1 - y if other else y, c)
        send(ref, 1 + ph, twin_r.at[ph, r % NZ], twin, ("twin", ph, r % NZ, other))

    def twin_wait(ph, r):
        landed(bufs[ph].at[pl.ds(0, 2)], twin_r.at[ph, r % NZ], ("twin", ph, r % NZ))

    def begin(ph):
        if ph == 1:
            landed(go_ref.at[0], in_sem.at[4], ("in", 0))
            go_ref[me] = jnp.concatenate([wo_ref[...].astype(F32), co_ref[...].astype(F32)], axis=0).astype(BF16)
        y_send(ph, 1, 0)
        for pi in (0, 1):
            for way in (0, 1):
                ring_send(ph, pi, way, 0)
        y_send(ph, 0, 0)
        twin_send(ph, 0, 0)

    def begin_other(ph):
        y_wait(ph, 1, 0)
        for way in (0, 1):
            ring_send(ph, 2, way, 0)

    def ring_step(ph, pi, s, way):
        ring_wait(ph, pi, way, s)
        r = -(s + 1) if way == 0 else s + 1
        if s < 3:
            ring_send(ph, pi, way, s + 1)
            if pi == 0:
                y_send(ph, 0, r)
            if pi == 1:
                twin_send(ph, r, 0)
        elif pi == 0:
            y_send(ph, 0, 4, way)

    def y_done(ph, r):
        y_wait(ph, 0, r)
        twin_send(ph, r, 1)

    def project_rel(r):
        twin_wait(0, r)
        project(zrel(r), gq_ref, lt_ref, ltt_ref, p_ref, dp_ref)

    def out_group(k):
        for r in OUT_GROUPS[k]:
            twin_wait(1, r)
        grad_times_out([zrel(r) for r in OUT_GROUPS[k]], k == 0, go_ref, gt_ref, u_ref, uc_ref)

    first_head = (9 * zrel(4)) // 2

    def head_group(k):
        first = first_head + 5 + sum(GROUPS[:k])
        attend_heads([(first + j) % HEADS for j in range(GROUPS[k])], p_ref, dp_ref, at_ref, dat_ref)

    def load_rest():
        landed(go_ref, in_sem.at[1], ("in", 0))
        landed(gain_ref, in_sem.at[2], ("in", 0))
        landed(cost_ref, in_sem.at[3], ("in", 0))
        normalize(x_ref, t_ref, g_ref, gain_ref, cost_ref, lt_ref, ltt_ref, gt_ref, res_ref)

    def run(op):
        kind = op[0]
        if kind in "BAX":
            ring_step(int(op[1]), "BAX".index(kind), int(op[2]), "ud".index(op[3]))
        elif kind == "b":
            begin(int(op[1]))
        elif kind == "x":
            begin_other(int(op[1]))
        elif kind == "Y":
            y_done(int(op[1]), int(op[3:]))
        elif kind == "T":
            twin_send(int(op[1]), 4, 0)
        elif kind == "P":
            project_rel(int(op[1:]))
        elif kind == "H":
            head_group(int(op[1:]))
        elif kind == "U":
            out_group(int(op[1]))
        elif kind == "N":
            load_rest()

    landed(gq_ref.at[0], in_sem.at[0], ("in", 0))
    gq_ref[me] = jnp.concatenate([wq_ref[...].astype(F32), cq_ref[...].astype(F32)], axis=0).astype(BF16)
    pl.semaphore_wait(barrier, 4 + NCKPT - 1)
    for op in ORDER:
        run(op)
    mine_ref[...] = out_scores(at_ref, dat_ref, u_ref, uc_ref) + res_ref[...]

    for k in range(1, NCKPT):
        remote(mine_ref, sums_ref.at[k], sent.at[3], sum_r.at[k], {"ckpt": (ck + k) % NCKPT}, ("sum", 0, k))
    landed(gq_ref.at[pl.ds(0, 20)], sent.at[0], ("sent", 0))
    landed(gq_ref.at[pl.ds(0, 16)], sent.at[1], ("sent", 1))
    landed(go_ref.at[pl.ds(0, 16)], sent.at[2], ("sent", 2))
    total = mine_ref[...]
    for k in range(1, NCKPT):
        landed(sums_ref.at[k], sum_r.at[k], ("sum", 0, k))
        total = total + sums_ref[k]
    out_ref[...] = total
    landed(sums_ref.at[pl.ds(1, NCKPT - 1)], sent.at[3], ("sent", 3))


def per_device(states, state_tangent, loss_grad, norm_gain, gain_costate, qkv_weight, qkv_costate, out_weight, out_costate):
    hbm = pl.BlockSpec(memory_space=pltpu.HBM)
    vmem = pl.BlockSpec(memory_space=pltpu.VMEM)
    out = pl.pallas_call(
        kernel,
        out_shape=jax.ShapeDtypeStruct((1, SEQ), F32),
        in_specs=[hbm] * 9,
        out_specs=vmem,
        scratch_shapes=[
            pltpu.VMEM((SEQ, D), BF16),
            pltpu.VMEM((SEQ, D), BF16),
            pltpu.VMEM((SEQ, D), BF16),
            pltpu.VMEM((1, D), BF16),
            pltpu.VMEM((1, D), BF16),
            pltpu.VMEM((72, D), BF16),
            pltpu.VMEM((72, D), BF16),
            pltpu.VMEM((24, D), BF16),
            pltpu.VMEM((24, D), BF16),
            pltpu.VMEM((NDEV, RQ, D), BF16),
            pltpu.VMEM((NDEV, RO, D), BF16),
            pltpu.VMEM((D, SEQ), BF16),
            pltpu.VMEM((D, SEQ), BF16),
            pltpu.VMEM((D, SEQ), BF16),
            pltpu.VMEM((1, SEQ), F32),
            pltpu.VMEM((3 * D, SEQ), BF16),
            pltpu.VMEM((3 * D, SEQ), BF16),
            pltpu.VMEM((D, SEQ), BF16),
            pltpu.VMEM((D, SEQ), BF16),
            pltpu.VMEM((D, SEQ), F32),
            pltpu.VMEM((D, SEQ), F32),
            pltpu.VMEM((1, SEQ), F32),
            pltpu.VMEM((NCKPT, 1, SEQ), F32),
            pltpu.SemaphoreType.DMA((5,)),
            pltpu.SemaphoreType.DMA((4,)),
            pltpu.SemaphoreType.DMA((2, 2, 4, 3)),
            pltpu.SemaphoreType.DMA((2, 9)),
            pltpu.SemaphoreType.DMA((2, NZ)),
            pltpu.SemaphoreType.DMA((NCKPT,)),
        ],
        compiler_params=pltpu.CompilerParams(
            collective_id=0, has_side_effects=True, vmem_limit_bytes=60 * 1024 * 1024
        ),
        cost_estimate=pl.CostEstimate(flops=9_000_000_000, bytes_accessed=3_000_000, transcendentals=3_200_000),
        name="scores",
    )(states, state_tangent, loss_grad, norm_gain, gain_costate, qkv_weight, qkv_costate, out_weight, out_costate)
    return out.reshape(SEQ)


def solution(mesh):
    return jax.shard_map(
        per_device,
        mesh=mesh,
        in_specs=(
            P("ckpt", "fsdp", None),
            P("ckpt", "fsdp", None),
            P("ckpt", "fsdp", None),
            P("ckpt", None),
            P("ckpt", None),
            P("ckpt", "fsdp", None),
            P("ckpt", "fsdp", None),
            P("ckpt", "fsdp", None),
            P("ckpt", "fsdp", None),
        ),
        out_specs=P("fsdp"),
        check_vma=False,
    )
```

```python
import functools
import math

import jax
import jax.numpy as jnp
from jax import lax
from jax.experimental import pallas as pl
from jax.experimental.pallas import tpu as pltpu
from jax.sharding import PartitionSpec as P

D = 768
HEADS = 12
HD = 64
SEQ = 512
EPSILON = 1e-05
NEGATIVE = -1e30
BF16 = jnp.bfloat16
F32 = jnp.float32
MESH = pl.DeviceIdType.MESH
NZ = 8
NCKPT = 8
NDEV = 32
RQ = 144
RO = 48

PIECES = (
    (("B", 64, 80, (64, 48), (112, 32)), ("A", 0, 64, (0, 32), (32, 32)), ("X", 0, 64, (0, 32), (32, 32))),
    (("B", 16, 32, (16, 16), (32, 16)), ("A", 0, 16, (0, 16), None), ("X", 0, 16, None, (0, 16))),
)


OUT_GROUPS = ((0, -1, 1), (-2, 2), (3, -3), (4,))
GROUPS = (2, 3, 2, 5)
ORDER = (
    "b1", "b0", "x1", "Y1_0", "x0", "B00u", "A00u", "B00d", "B10d", "A10d", "A00d", "Y0_0",
    "X00u", "Y0_-1", "X00d", "Y0_1", "B01u", "B01d", "N", "X10d", "B10u", "P0", "A01u", "X01u",
    "P1", "Y0_-2", "A10u", "B02u", "X01d", "Y0_2", "Y1_1", "X10u", "B02d", "A01d", "Y1_-1", "B11u",
    "P-1", "A02u", "B11d", "P2", "A11d", "X11d", "U0", "X02u", "Y0_-3", "X02d", "P-2", "A11u",
    "B03d", "P-3", "A02d", "B03u", "Y0_3", "H0", "B12d", "X11u", "A12d", "B12u", "Y1_-2", "Y1_2",
    "X12d", "P3", "H2", "A03u", "X03u", "U1", "B13d", "A12u", "A13d", "X03d", "Y0_4", "A03d",
    "T0", "X13d", "B13u", "H1", "X12u", "X13u", "Y1_3", "P4", "Y1_4", "Y1_-3", "A13u", "T1",
    "H3", "U3", "U2",
)


def remote(src, dst, ssem, rsem, where, tag):
    copy = pltpu.make_async_remote_copy(
        src_ref=src, dst_ref=dst, send_sem=ssem, recv_sem=rsem, device_id=where, device_id_type=MESH
    )
    copy.start()
    return copy


def landed(ref, sem, tag):
    pltpu.make_async_copy(ref, ref, sem).wait()


def dot(a, b):
    return lax.dot_general(a, b, (((1,), (0,)), ((), ())), preferred_element_type=F32)


def normalize(x_ref, t_ref, g_ref, gain_ref, cost_ref, lt_ref, ltt_ref, gt_ref, res_ref):
    gain = gain_ref[...].astype(F32)
    cost = cost_ref[...].astype(F32)

    def body(i, carry):
        rows = pl.ds(pl.multiple_of(i * 128, 128), 128)
        x = x_ref[rows, :].astype(F32)
        t = t_ref[rows, :].astype(F32)
        g = g_ref[rows, :].astype(F32)
        inv = lax.rsqrt(jnp.mean(x * x, axis=1, keepdims=True) + EPSILON)
        normed = x * inv
        cross = jnp.mean(x * t, axis=1, keepdims=True)
        normed_t = t * inv - x * (inv * inv * inv) * cross
        lifted = (gain * normed).astype(BF16)
        lifted_t = (cost * normed + gain * normed_t).astype(BF16)
        lt_ref[:, rows] = lifted.T
        ltt_ref[:, rows] = lifted_t.T
        gt_ref[:, rows] = g_ref[rows, :].T
        p = g * t
        q = p[:, 0:128]
        for k in range(1, D // 128):
            q = q + p[:, 128 * k : 128 * k + 128]
        res_ref[:, rows] = jnp.sum(q.T, axis=0, keepdims=True)
        return carry

    lax.fori_loop(0, SEQ // 128, body, 0)


def project(zc, gq_ref, lt_ref, ltt_ref, p_ref, dp_ref):
    devs = pl.ds(zc * 4, 4)
    r1 = dot(gq_ref[devs].reshape(4 * RQ, D), lt_ref[...]).reshape(4, RQ, SEQ)
    r2 = dot(gq_ref[devs, 0:80, :].reshape(320, D), ltt_ref[...]).reshape(4, 80, SEQ)
    rows = pl.ds(pl.multiple_of(zc * 288, 288), 288)
    p_ref[rows, :] = r1[:, 0:72].reshape(288, SEQ).astype(BF16)
    dp_ref[rows, :] = (r2[:, 0:72] + r1[:, 72:144]).reshape(288, SEQ).astype(BF16)


def head_operands(h, p_ref, dp_ref):
    def rows(base):
        return pl.ds(pl.multiple_of(base + h * HD, HD), HD)

    q, dq = p_ref[rows(0), :], dp_ref[rows(0), :]
    k, dk = p_ref[rows(D), :], dp_ref[rows(D), :]
    v, dv = p_ref[rows(2 * D), :], dp_ref[rows(2 * D), :]
    kd = jnp.concatenate([k, dk], axis=0).T
    scale = BF16(1.0 / math.sqrt(HD))
    q, dq = q * scale, dq * scale
    rhs_s = jnp.concatenate([q, jnp.zeros_like(q)], axis=0)
    rhs_d = jnp.concatenate([dq, q], axis=0)
    return rows(0), kd, rhs_s, rhs_d, v, jnp.concatenate([v, dv], axis=0)


def softmax_block(s, d, upper):
    n = s.shape[0]
    diag = jnp.where(upper, s[n - 128 :], NEGATIVE)
    s = diag if n == 128 else jnp.concatenate([s[: n - 128], diag], axis=0)
    m = jnp.max(s, axis=0, keepdims=True)
    e = jnp.exp2((s - m) * math.log2(math.e))
    a = e * (1.0 / jnp.sum(e, axis=0, keepdims=True))
    t = jnp.sum(a * d, axis=0, keepdims=True)
    return a.astype(BF16), (a * (d - t)).astype(BF16)


def attend_heads(hs, p_ref, dp_ref, at_ref, dat_ref):
    row = lax.broadcasted_iota(jnp.int32, (128, 128), 0)
    col = lax.broadcasted_iota(jnp.int32, (128, 128), 1)
    upper = row <= col
    operands = [head_operands(h, p_ref, dp_ref) for h in hs]
    empty = jnp.zeros((128, 128), BF16)
    for b in (1, 0):
        cols = slice(256 * b, 256 * b + 256)
        n = 256 * (b + 1)
        logits = [(dot(kd[:n], rs[:, cols]), dot(kd[:n], rd[:, cols])) for _, kd, rs, rd, _, _ in operands]
        weights = []
        for s, d in logits:
            left = softmax_block(s[: n - 128, :128], d[: n - 128, :128], upper)
            right = softmax_block(s[:, 128:], d[:, 128:], upper)
            weights.append(
                [jnp.concatenate([jnp.concatenate([l, empty], axis=0), r], axis=1) for l, r in zip(left, right)]
            )
        for (rows, _, _, _, v, vv), (a, da) in zip(operands, weights):
            o1 = dot(vv[:, :n], a)
            o2 = dot(v[:, :n], da)
            at_ref[rows, cols] = o1[:HD].astype(BF16)
            dat_ref[rows, cols] = (o1[HD:] + o2).astype(BF16)


def grad_times_out(zcs, first, go_ref, gt_ref, u_ref, uc_ref):
    blocks = [go_ref[pl.ds(zc * 4, 4)].astype(F32) for zc in zcs]
    grad = jnp.concatenate([gt_ref[pl.ds(pl.multiple_of(zc * 96, 96), 96), :] for zc in zcs], axis=0)
    for lo, ref in ((0, u_ref), (24, uc_ref)):
        w = jnp.concatenate([b[:, lo : lo + 24].reshape(96, D) for b in blocks], axis=0).astype(BF16)
        term = dot(w.T, grad)
        ref[...] = term if first else ref[...] + term


def out_scores(at_ref, dat_ref, u_ref, uc_ref):
    total = jnp.zeros((1, SEQ), F32)
    for i in range(0, D, 128):
        rows = slice(i, i + 128)
        term = dat_ref[rows, :].astype(F32) * u_ref[rows, :] + at_ref[rows, :].astype(F32) * uc_ref[rows, :]
        total = total + jnp.sum(term, axis=0, keepdims=True)
    return total


def kernel(
    x_hbm, t_hbm, g_hbm, gain_hbm, cost_hbm, wq_hbm, cq_hbm, wo_hbm, co_hbm,
    out_ref,
    x_ref, t_ref, g_ref, gain_ref, cost_ref, wq_ref, cq_ref, wo_ref, co_ref,
    gq_ref, go_ref, lt_ref, ltt_ref, gt_ref, res_ref, p_ref, dp_ref, at_ref, dat_ref, u_ref, uc_ref,
    mine_ref, sums_ref,
    in_sem, sent, ring_r, y_r, twin_r, sum_s, sum_r,
):
    ck = lax.axis_index("ckpt")
    me = lax.axis_index("fsdp")
    z = me // 4
    y = (me // 2) % 2
    c = me % 2

    def dev(zz, yy, cc):
        return zz * 4 + yy * 2 + cc

    def zrel(r):
        return (z + (r + NZ)) % NZ

    up = dev(zrel(1), y, c)
    down = dev(zrel(-1), y, c)
    side = dev(z, 1 - y, c)
    twin = dev(z, y, 1 - c)

    barrier = pltpu.get_barrier_semaphore()
    for peer in (up, down, side, twin):
        pl.semaphore_signal(barrier, inc=1, device_id={"fsdp": peer}, device_id_type=MESH)
    for i, src, dst in (
        (0, wq_hbm.at[0], wq_ref), (5, cq_hbm.at[0], cq_ref), (4, wo_hbm.at[0], wo_ref), (6, co_hbm.at[0], co_ref),
    ):
        pltpu.make_async_copy(src, dst, in_sem.at[i]).start()
    for k in range(1, NCKPT):
        pl.semaphore_signal(barrier, inc=1, device_id={"ckpt": (ck + k) % NCKPT}, device_id_type=MESH)
    for i, src, dst in (
        (1, x_hbm.at[0], x_ref), (1, t_hbm.at[0], t_ref), (1, g_hbm.at[0], g_ref),
        (2, gain_hbm, gain_ref), (3, cost_hbm, cost_ref),
    ):
        pltpu.make_async_copy(src, dst, in_sem.at[i]).start()

    bufs = (gq_ref, go_ref)

    def send(ref, slot, rsem, peer, tag):
        remote(ref, ref, sent.at[slot], rsem, {"fsdp": peer}, tag)

    def part(ph, r, yy, cc, first, count):
        return bufs[ph].at[dev(zrel(r), yy, cc), pl.ds(first, count), :]

    def whole(ph, r, yy, cc):
        return bufs[ph].at[dev(zrel(r), yy, cc)]

    def owner_y(kind):
        return 1 - y if kind == "X" else y

    def hop_rows(piece, way, s):
        kind, first, count, last_up, last_down = piece
        if s < 3:
            return (first, count)
        return last_up if way == 0 else last_down

    def ring_send(ph, pi, way, s):
        piece = PIECES[ph][pi]
        span = hop_rows(piece, way, s)
        if span is None:
            return
        r = -s if way == 0 else s
        ref = part(ph, r, owner_y(piece[0]), c, *span)
        send(ref, 0, ring_r.at[ph, way, s, pi], up if way == 0 else down, ("ring", ph, pi, way, s))

    def ring_wait(ph, pi, way, s):
        piece = PIECES[ph][pi]
        span = hop_rows(piece, way, s)
        if span is None:
            return
        r = -(s + 1) if way == 0 else s + 1
        landed(part(ph, r, owner_y(piece[0]), c, *span), ring_r.at[ph, way, s, pi], ("ring", ph, pi, way, s))

    def y_rows(ph, pi, r, half):
        _, first, count, last_up, last_down = PIECES[ph][pi]
        return (first, count) if half is None else (last_up, last_down)[half]

    def y_slot(pi, r):
        return 8 if pi == 1 else r % NZ

    def y_send(ph, pi, r, half=None):
        slot = y_slot(pi, r)
        ref = part(ph, r, y, c, *y_rows(ph, pi, r, half))
        send(ref, 0, y_r.at[ph, slot], side, ("y", ph, slot))

    def y_wait(ph, pi, r):
        slot = y_slot(pi, r)
        landed(part(ph, r, 1 - y, c, *y_rows(ph, pi, r, None)), y_r.at[ph, slot], ("y", ph, slot))

    def twin_send(ph, r, other):
        ref = whole(ph, r, 1 - y if other else y, c)
        send(ref, 1 + ph, twin_r.at[ph, r % NZ], twin, ("twin", ph, r % NZ, other))

    def twin_wait(ph, r):
        landed(bufs[ph].at[pl.ds(0, 2)], twin_r.at[ph, r % NZ], ("twin", ph, r % NZ))

    def begin(ph):
        if ph == 1:
            landed(wo_ref, in_sem.at[4], ("in", 0))
            landed(co_ref, in_sem.at[6], ("in", 0))
            go_ref[me] = jnp.concatenate([wo_ref[...].astype(F32), co_ref[...].astype(F32)], axis=0).astype(BF16)
        y_send(ph, 1, 0)
        for pi in (0, 1):
            for way in (0, 1):
                ring_send(ph, pi, way, 0)
        y_send(ph, 0, 0)
        twin_send(ph, 0, 0)

    def begin_other(ph):
        y_wait(ph, 1, 0)
        for way in (0, 1):
            ring_send(ph, 2, way, 0)

    def ring_step(ph, pi, s, way):
        ring_wait(ph, pi, way, s)
        r = -(s + 1) if way == 0 else s + 1
        if s < 3:
            ring_send(ph, pi, way, s + 1)
            if pi == 0:
                y_send(ph, 0, r)
            if pi == 1:
                twin_send(ph, r, 0)
        elif pi == 0:
            y_send(ph, 0, 4, way)

    def y_done(ph, r):
        y_wait(ph, 0, r)
        twin_send(ph, r, 1)

    def project_rel(r):
        twin_wait(0, r)
        project(zrel(r), gq_ref, lt_ref, ltt_ref, p_ref, dp_ref)

    def out_group(k):
        for r in OUT_GROUPS[k]:
            twin_wait(1, r)
        grad_times_out([zrel(r) for r in OUT_GROUPS[k]], k == 0, go_ref, gt_ref, u_ref, uc_ref)

    first_head = (9 * zrel(4)) // 2

    def head_group(k):
        first = first_head + 5 + sum(GROUPS[:k])
        attend_heads([(first + j) % HEADS for j in range(GROUPS[k])], p_ref, dp_ref, at_ref, dat_ref)

    def load_rest():
        landed(go_ref, in_sem.at[1], ("in", 0))
        landed(gain_ref, in_sem.at[2], ("in", 0))
        landed(cost_ref, in_sem.at[3], ("in", 0))
        normalize(x_ref, t_ref, g_ref, gain_ref, cost_ref, lt_ref, ltt_ref, gt_ref, res_ref)

    def run(op):
        kind = op[0]
        if kind in "BAX":
            ring_step(int(op[1]), "BAX".index(kind), int(op[2]), "ud".index(op[3]))
        elif kind == "b":
            begin(int(op[1]))
        elif kind == "x":
            begin_other(int(op[1]))
        elif kind == "Y":
            y_done(int(op[1]), int(op[3:]))
        elif kind == "T":
            twin_send(int(op[1]), 4, 0)
        elif kind == "P":
            project_rel(int(op[1:]))
        elif kind == "H":
            head_group(int(op[1:]))
        elif kind == "U":
            out_group(int(op[1]))
        elif kind == "N":
            load_rest()

    landed(wq_ref, in_sem.at[0], ("in", 0))
    landed(cq_ref, in_sem.at[5], ("in", 0))
    gq_ref[me] = jnp.concatenate([wq_ref[...].astype(F32), cq_ref[...].astype(F32)], axis=0).astype(BF16)
    pl.semaphore_wait(barrier, 4 + NCKPT - 1)
    for op in ORDER:
        run(op)
    mine_ref[...] = out_scores(at_ref, dat_ref, u_ref, uc_ref) + res_ref[...]

    for k in range(1, NCKPT):
        remote(mine_ref, sums_ref.at[k], sum_s.at[k], sum_r.at[k], {"ckpt": (ck + k) % NCKPT}, ("sum", 0, k))
    landed(gq_ref.at[pl.ds(0, 20)], sent.at[0], ("sent", 0))
    landed(gq_ref.at[pl.ds(0, 16)], sent.at[1], ("sent", 1))
    landed(go_ref.at[pl.ds(0, 16)], sent.at[2], ("sent", 2))
    total = mine_ref[...]
    for k in range(1, NCKPT):
        landed(sums_ref.at[k], sum_r.at[k], ("sum", 0, k))
        total = total + sums_ref[k]
    out_ref[...] = total
    for k in range(1, NCKPT):
        landed(mine_ref, sum_s.at[k], ("sent", 3))


def per_device(states, state_tangent, loss_grad, norm_gain, gain_costate, qkv_weight, qkv_costate, out_weight, out_costate):
    hbm = pl.BlockSpec(memory_space=pltpu.HBM)
    vmem = pl.BlockSpec(memory_space=pltpu.VMEM)
    out = pl.pallas_call(
        kernel,
        out_shape=jax.ShapeDtypeStruct((1, SEQ), F32),
        in_specs=[hbm] * 9,
        out_specs=vmem,
        scratch_shapes=[
            pltpu.VMEM((SEQ, D), BF16),
            pltpu.VMEM((SEQ, D), BF16),
            pltpu.VMEM((SEQ, D), BF16),
            pltpu.VMEM((1, D), BF16),
            pltpu.VMEM((1, D), BF16),
            pltpu.VMEM((72, D), BF16),
            pltpu.VMEM((72, D), BF16),
            pltpu.VMEM((24, D), BF16),
            pltpu.VMEM((24, D), BF16),
            pltpu.VMEM((NDEV, RQ, D), BF16),
            pltpu.VMEM((NDEV, RO, D), BF16),
            pltpu.VMEM((D, SEQ), BF16),
            pltpu.VMEM((D, SEQ), BF16),
            pltpu.VMEM((D, SEQ), BF16),
            pltpu.VMEM((1, SEQ), F32),
            pltpu.VMEM((3 * D, SEQ), BF16),
            pltpu.VMEM((3 * D, SEQ), BF16),
            pltpu.VMEM((D, SEQ), BF16),
            pltpu.VMEM((D, SEQ), BF16),
            pltpu.VMEM((D, SEQ), F32),
            pltpu.VMEM((D, SEQ), F32),
            pltpu.VMEM((1, SEQ), F32),
            pltpu.VMEM((NCKPT, 1, SEQ), F32),
            pltpu.SemaphoreType.DMA((7,)),
            pltpu.SemaphoreType.DMA((3,)),
            pltpu.SemaphoreType.DMA((2, 2, 4, 3)),
            pltpu.SemaphoreType.DMA((2, 9)),
            pltpu.SemaphoreType.DMA((2, NZ)),
            pltpu.SemaphoreType.DMA((NCKPT,)),
            pltpu.SemaphoreType.DMA((NCKPT,)),
        ],
        compiler_params=pltpu.CompilerParams(
            collective_id=0, has_side_effects=True, vmem_limit_bytes=60 * 1024 * 1024
        ),
        cost_estimate=pl.CostEstimate(flops=9_000_000_000, bytes_accessed=3_000_000, transcendentals=3_200_000),
        name="scores",
    )(states, state_tangent, loss_grad, norm_gain, gain_costate, qkv_weight, qkv_costate, out_weight, out_costate)
    return out.reshape(SEQ)


def solution(mesh):
    return jax.shard_map(
        per_device,
        mesh=mesh,
        in_specs=(
            P("ckpt", "fsdp", None),
            P("ckpt", "fsdp", None),
            P("ckpt", "fsdp", None),
            P("ckpt", None),
            P("ckpt", None),
            P("ckpt", "fsdp", None),
            P("ckpt", "fsdp", None),
            P("ckpt", "fsdp", None),
            P("ckpt", "fsdp", None),
        ),
        out_specs=P("fsdp"),
        check_vma=False,
    )
```
